256 devices in a mesh: dp: 8 (over x_hi, y), ctx: 32 (over x_lo, z, core).
Axes of the slice: x: 4 (x_hi: 2, x_lo: 2; x = x_hi * 2 + x_lo), y: 4, z: 8, core: 2. Of those that a mesh axis runs over, the one named last changes fastest.
Arguments:
- query_nope: bfloat16 [4096, 8192], P('ctx', 'dp'), may hold values from -6 to 6
- query_rope: bfloat16 [4096, 4096], P('ctx', 'dp'), may hold values from -6 to 6
- latent: bfloat16 [4096, 512], P('ctx'), may hold values from -120 to 120
- rope_key: bfloat16 [4096, 64], P('ctx'), may hold values from -6 to 6
- grad_out: bfloat16 [4096, 32768], P('ctx', 'dp'), may hold values from -6 to 6
- saved_out: bfloat16 [4096, 32768], P('ctx', 'dp'), may hold values from -3 to 3
- up_key: bfloat16 [8192, 512], P(('dp', 'ctx')), may hold values from -0.5 to 0.5
Outputs:
- latent_grad: float32 [4096, 512], P('ctx')
- rope_key_grad: float32 [4096, 64], P('ctx')
- query_nope_grad: bfloat16 [4096, 8192], P('ctx', 'dp')
- query_rope_grad: bfloat16 [4096, 4096], P('ctx', 'dp')
- up_key_grad: float32 [8192, 512], P(('dp', 'ctx'))
The draws below stay inside these ranges and needn't reach their ends.
All inputs are finite; a program needn't handle non-finite values.
Results may differ from the reference program's by a relative error of at most 0.03.
Values may be sent and summed in bfloat16 or wider, within the bound.
No kernel may reach another device: no remote copies, remote signals or barrier semaphores. Data moves between devices by JAX's collectives and lax.ppermute only.
A program may use at most 128 MiB of HBM per device.

```python
import math
import jax
import jax.numpy as jnp
from jax import lax

HEADS = 64
NOPE = 128
ROPE = 64
LATENT = 512
TOK_DEV = 128
SEQ = 4096
N_CTX = 32


def draw_latent(key, part):
    key = jax.random.fold_in(key, 7)
    values = jax.random.normal(key, (SEQ, LATENT), jnp.float32)
    values = jnp.clip(values, -5.0, 5.0)
    return values.astype(jnp.bfloat16)


def with_spikes(result, stream_key, source, target, blocks, factor):
    owner, partner = [(jnp.arange(result.shape[dim]) // (result.shape[dim] // blocks)).reshape([-1 if axis == dim else 1 for axis in range(result.ndim)]) for dim in (source, target)]
    chosen = jax.random.permutation(stream_key, blocks)[partner]
    strong = (owner == chosen) | (owner == (partner + blocks // 2) % blocks)
    return jnp.where(strong, factor * result, result)


def block_levels(stream_key, extent, cuts, low, high):
    level, own = 1.0, jax.random.fold_in(stream_key, 6)
    for dim, blocks in cuts:
        draws = jnp.exp(jax.random.uniform(jax.random.fold_in(own, dim), (blocks,), jnp.float32, low / len(cuts), high / len(cuts)))
        level = level * jnp.repeat(draws, extent[dim] // blocks).reshape([-1 if axis == dim else 1 for axis in range(len(extent))])
    return level


def gaussian(rng, dims, scale, limit, split=(), kind=jnp.bfloat16):
    result = scale * jax.random.normal(rng, dims, jnp.float32)
    if split:
        result = result * block_levels(rng, dims, split, -0.22, 0.18)
    return jnp.clip(result, -limit, limit).astype(kind)


def gaussian_with(rng, shape, width, reach, split, heavy, kind=jnp.bfloat16):
    array = width * jax.random.normal(rng, shape, jnp.float32)
    if split:
        array = array * block_levels(rng, shape, split, -0.22, 0.18)
    return jnp.clip(with_spikes(array, jax.random.fold_in(rng, 3), *heavy), -reach, reach).astype(kind)


def setup_inputs(seed: int = 0) -> dict:
    seeds = jax.random.split(jax.random.key(seed), 8)
    return {
        "query_nope": gaussian_with(seeds[0], (SEQ, HEADS * NOPE), 1.0, 6.0, ((0, 32), (1, 8)), (0, 1, 32, 2.75)),
        "query_rope": gaussian(seeds[1], (SEQ, HEADS * ROPE), 1.0, 6.0, ((0, 32), (1, 8))),
        "latent": draw_latent(jax.random.fold_in(seeds[7], 71), 0),
        "rope_key": gaussian(seeds[3], (SEQ, ROPE), 1.0, 6.0, ((0, 32),)),
        "grad_out": gaussian(seeds[4], (SEQ, HEADS * LATENT), 1.0, 6.0, ((0, 32), (1, 8))),
        "saved_out": gaussian(seeds[5], (SEQ, HEADS * LATENT), 0.5, 3.0, ((0, 32), (1, 8))),
        "up_key": gaussian(seeds[6], (HEADS * NOPE, LATENT), NOPE ** -0.5, 0.5, ((0, 256),)),
    }


def positions():
    stored_index = jnp.arange(SEQ, dtype=jnp.int32)
    owner_device = stored_index // TOK_DEV
    local_index = stored_index % TOK_DEV
    half_rows = TOK_DEV // 2
    late_position = (2 * N_CTX - 1 - owner_device) * half_rows + local_index - half_rows
    return jnp.where(local_index < half_rows, owner_device * half_rows + local_index, late_position)

def rounded(values):
    return lax.optimization_barrier(values.astype(jnp.bfloat16)).astype(jnp.float32)

def reference(query_nope, query_rope, latent, rope_key, grad_out, saved_out, up_key):
    score_scale = 1.0 / math.sqrt(NOPE + ROPE)
    position = positions()
    allowed = position[None, :] <= position[:, None]
    weights = up_key.astype(jnp.float32).reshape(HEADS, NOPE, LATENT)
    group_size = math.gcd(HEADS, 4)
    groups = HEADS // group_size
    key_width = LATENT + ROPE
    nope_heads = query_nope.astype(jnp.float32).reshape(SEQ, HEADS, NOPE)
    query_latent = rounded(jnp.einsum('shn,hnl->hsl', nope_heads, weights))
    rope_heads = query_rope.astype(jnp.float32).reshape(SEQ, HEADS, ROPE).transpose(1, 0, 2)
    query_full = jnp.concatenate([query_latent, rope_heads], axis=2)
    key_rows = jnp.concatenate([latent, rope_key], axis=1).astype(jnp.float32)
    grad_heads = grad_out.astype(jnp.float32).reshape(SEQ, HEADS, LATENT).transpose(1, 0, 2)
    out_heads = saved_out.astype(jnp.float32).reshape(SEQ, HEADS, LATENT).transpose(1, 0, 2)
    row_delta = lax.optimization_barrier(jnp.sum(grad_heads * out_heads, axis=2))

    def per_group(pieces):
        query_part, grad_part, delta_part = pieces
        scores = score_scale * jnp.einsum('gsc,kc->gsk', query_part, key_rows)
        scores = jnp.where(allowed[None], scores, -jnp.inf)
        row_top = lax.optimization_barrier(jnp.max(scores, axis=2, keepdims=True))
        log_total = row_top + jnp.log(lax.optimization_barrier(jnp.sum(jnp.exp(scores - row_top), axis=2, keepdims=True)))
        probability = jnp.exp(scores - log_total)
        prob_rounded = rounded(probability)
        prob_grad = jnp.einsum('gsl,kl->gsk', grad_part, key_rows[:, :LATENT])
        score_grad = rounded(probability * (prob_grad - delta_part[:, :, None]))
        key_grads = score_scale * jnp.einsum('gsk,gsc->kc', score_grad, query_part)
        value_side = jnp.einsum('gsk,gsl->kl', prob_rounded, grad_part)
        key_grads = key_grads + jnp.concatenate([value_side, jnp.zeros((SEQ, ROPE), jnp.float32)], axis=1)
        query_grads = score_scale * jnp.einsum('gsk,kc->gsc', score_grad, key_rows)
        return (key_grads, query_grads)
    pieces = (query_full.reshape(groups, group_size, SEQ, key_width), grad_heads.reshape(groups, group_size, SEQ, LATENT), row_delta.reshape(groups, group_size, SEQ))
    key_grads, query_grads = lax.map(per_group, pieces)
    key_grads = lax.optimization_barrier(jnp.sum(key_grads, axis=0))
    query_grads = query_grads.reshape(HEADS, SEQ, key_width)
    query_latent_grad = rounded(query_grads[:, :, :LATENT])
    rope_grad = query_grads[:, :, LATENT:].transpose(1, 0, 2).reshape(SEQ, HEADS * ROPE).astype(jnp.bfloat16)
    nope_grad = jnp.einsum('hsl,hnl->shn', query_latent_grad, weights).reshape(SEQ, HEADS * NOPE).astype(jnp.bfloat16)
    weight_term = jnp.einsum('shn,hsl->hnl', nope_heads, query_latent_grad).reshape(HEADS * NOPE, LATENT)
    return (key_grads[:, :LATENT], key_grads[:, LATENT:], nope_grad, rope_grad, weight_term)
```

```python
import math

import jax
import jax.numpy as jnp
from jax import lax
from jax.experimental import pallas as pl
from jax.experimental.pallas import tpu as pltpu
from jax.sharding import Mesh
from jax.sharding import PartitionSpec as P

NOPE = 128
ROPE = 64
LAT = 512
HEADS = 8
HALF = 64
ROWS = HEADS * HALF
WIDE = 640
PACK = 704
GRAD = 576
SCALE = 1.0 / math.sqrt(NOPE + ROPE)
LOG2E = math.log2(math.e)
LOW = -1e30
BF = jnp.bfloat16
F32 = jnp.float32
GROUPS = ((4, 3, 5, 2), (6, 1, 7, 0))
VMEM_LIMIT = 48 * 1024 * 1024


def dot(a, b):
    return lax.dot_general(a, b, (((1,), (0,)), ((), ())), preferred_element_type=F32)


def dot_nt(a, b):
    return lax.dot_general(a, b, (((1,), (1,)), ((), ())), preferred_element_type=F32)


def call(kernel, outs, count, scratch=(), flops=0, smem=0):
    vm = pl.BlockSpec(memory_space=pltpu.VMEM)
    sm = pl.BlockSpec(memory_space=pltpu.SMEM)
    return pl.pallas_call(
        kernel,
        out_shape=[jax.ShapeDtypeStruct(s, d) for s, d in outs],
        in_specs=[sm] * smem + [vm] * count,
        out_specs=[vm] * len(outs),
        scratch_shapes=list(scratch),
        compiler_params=pltpu.CompilerParams(vmem_limit_bytes=VMEM_LIMIT),
        cost_estimate=pl.CostEstimate(flops=flops, bytes_accessed=4_000_000, transcendentals=0),
    )


def pack_kernel(lat, rope, w, out):
    for j in range(4):
        cols = pl.ds(128 * j, 128)
        out[pl.ds(128 * j, 128), :] = lat[:, cols]
        out[pl.ds(576 + 32 * j, 32), :] = w[:, cols]
    out[512:576, :] = jnp.concatenate([rope[0:HALF, :], rope[HALF : 2 * HALF, :]], axis=1)


def prep_kernel(g_own, g_oth, qr_own, qr_oth, o_own, g_out, qr_out, delta):
    for p, (g, qr) in enumerate(((g_own, qr_own), (g_oth, qr_oth))):
        for part in range(2):
            rows = pl.ds(part * HALF, HALF)
            for h in range(HEADS):
                g_out[part, p, pl.ds(h * HALF, HALF), :] = g[rows, pl.ds(h * LAT, LAT)]
            for k in range(HEADS // 2):
                pair = qr[rows, pl.ds(128 * k, 128)]
                zero = jnp.zeros((HALF, ROPE), BF)
                qr_out[part, p, pl.ds(2 * k * HALF, HALF), :] = jnp.concatenate(
                    [pair[:, :ROPE], zero], axis=1
                )
                qr_out[part, p, pl.ds((2 * k + 1) * HALF, HALF), :] = jnp.concatenate(
                    [pair[:, ROPE:], zero], axis=1
                )
    for part in range(2):
        rows = pl.ds(part * HALF, HALF)
        for k in range(HEADS // 2):
            halves = []
            for h in (2 * k, 2 * k + 1):
                cols = pl.ds(h * LAT, LAT)
                prod = g_own[rows, cols].astype(F32) * o_own[rows, cols].astype(F32)
                halves.append(
                    prod[:, 0:128] + prod[:, 128:256] + prod[:, 256:384] + prod[:, 384:512]
                )
            both = jnp.concatenate(halves, axis=0).T
            delta[pl.ds(part, 1), pl.ds(128 * k, 128)] = jnp.sum(both, axis=0, keepdims=True)


def positions_of(info, p, group):
    core, z, xl = info[0], info[1], info[2]
    owner = 2 * (xl * 8 + z) + jnp.where(p == 0, core, 1 - core)
    keys = []
    for r in group:
        e = 2 * (xl * 8 + ((z + r) & 7)) + core
        keys.append((e * HALF, (63 - e) * HALF))
    return (owner * HALF, (63 - owner) * HALF), keys


def mask_of(first_row, key_rows):
    key = lax.broadcasted_iota(jnp.int32, (HALF, ROWS), 0)
    tok = lax.broadcasted_iota(jnp.int32, (HALF, ROWS), 1) & (HALF - 1)
    diff = key - tok
    return jnp.concatenate([diff <= first_row - k for k in key_rows], axis=0)


def stats_of(s):
    top = jnp.max(s, axis=0, keepdims=True)
    return top, jnp.sum(jnp.exp2(s - top), axis=0, keepdims=True)


def merge(a, b):
    top = jnp.maximum(a[0], b[0])
    return top, a[1] * jnp.exp2(a[0] - top) + b[1] * jnp.exp2(b[0] - top)


def forward_kernel(info, *refs):
    packs, refs = refs[:16], refs[16:]
    (w_oth, q_own, q_oth, qr, delta, kall, w_full, qf, stats) = refs
    core, z, xl = info[0], info[1], info[2]
    for gi, group in enumerate(GROUPS):
        for b, r in enumerate(group):
            for side in range(2):
                pack = packs[(gi * 4 + b) * 2 + side]
                rows = pl.ds(b * HALF, HALF)
                for j in range(4):
                    cols = pl.ds(128 * j, 128)
                    kall[gi, side, rows, cols] = pack[pl.ds(128 * j, HALF), :]
                    kall[gi, 2 + side, rows, cols] = pack[pl.ds(128 * j + HALF, HALF), :]
                ropes = pack[512:576, :]
                kall[gi, side, rows, 512:640] = ropes
                kall[gi, 2 + side, rows, 512:640] = jnp.concatenate(
                    [ropes[:, ROPE:], ropes[:, :ROPE]], axis=1
                )
                column = xl if side == 0 else 1 - xl
                chip = column * 8 + ((z + r) & 7)
                slot = (gi * 4 + b) * 2 + side
                own_row = pl.multiple_of((2 * chip + core) * 32, 32)
                oth_row = pl.multiple_of((2 * chip + 1 - core) * 32, 32)
                for j in range(4):
                    cols = pl.ds(128 * j, 128)
                    w_full[pl.ds(own_row, 32), cols] = pack[pl.ds(576 + 32 * j, 32), :]
                    w_full[pl.ds(oth_row, 32), cols] = w_oth[slot, pl.ds(32 * j, 32), :]
    for p, q in enumerate((q_own, q_oth)):
        for h in range(HEADS):
            lat = dot(q[:, pl.ds(h * NOPE, NOPE)], w_full[pl.ds(h * NOPE, NOPE), :]).astype(BF)
            qf[0, p, pl.ds(h * HALF, HALF), 0:512] = lat[:HALF]
            qf[1, p, pl.ds(h * HALF, HALF), 0:512] = lat[HALF:]
        for part in range(2):
            qf[part, p, :, 512:640] = qr[part, p]
    sel = 1 - xl
    sel_keys = jnp.where(xl == 0, 3, 1)
    factor = SCALE * LOG2E

    def step(p, carry):
        late = early = cross = None
        for gi, group in enumerate(GROUPS):
            firsts, keys = positions_of(info, p, group)
            for i in range(3):
                s = dot_nt(kall[gi, i], qf[1, p]) * factor
                if i == 2:
                    s = jnp.where(mask_of(firsts[1], [k[1] for k in keys]), s, LOW)
                now = stats_of(s)
                late = now if late is None else merge(late, now)
            s = dot_nt(kall[gi, 0], qf[0, p]) * factor
            now = stats_of(jnp.where(mask_of(firsts[0], [k[0] for k in keys]), s, LOW))
            early = now if early is None else merge(early, now)
            now = stats_of(dot_nt(kall[gi, sel_keys], qf[sel, p]) * factor)
            cross = now if cross is None else merge(cross, now)
        more_late, more_early = merge(late, cross), merge(early, cross)
        late = [jnp.where(sel == 1, a, b) for a, b in zip(more_late, late)]
        early = [jnp.where(sel == 0, a, b) for a, b in zip(more_early, early)]
        zero = jnp.zeros((2, ROWS), F32)
        stats[p] = jnp.concatenate([*early, *late, delta[...], zero], axis=0)
        return carry

    lax.fori_loop(0, 2, step, 0)


def backward_kernel(group, last, info, kall, qf, g, mine, theirs, *refs):
    if last:
        dq_in, out_own, out_oth, dq_own, dq_send, kt, dk, dq = refs
    else:
        out_own, out_oth, dq, kt, dk = refs
    xl = info[2]
    sel = 1 - xl
    sel_keys = jnp.where(xl == 0, 3, 1)
    factor = SCALE * LOG2E
    for i in range(4):
        kt[i] = kall[i].T
    dk[...] = jnp.zeros_like(dk)

    def add(p, part, i, lse, delta, mask):
        keys, queries, grads = kall[i], qf[part, p], g[part, p]
        prob = jnp.exp2(dot_nt(keys, queries) * factor - lse)
        if mask is not None:
            prob = jnp.where(mask, prob, 0.0)
        dprob = dot_nt(keys[:, :LAT], grads)
        ds = ((prob * SCALE) * (dprob - delta)).astype(BF)
        dk[i] += dot(ds, queries)
        dk[i, :, 0:LAT] += dot(prob.astype(BF), grads)
        return dot(kt[i], ds)

    def step(p, carry):
        firsts, keys = positions_of(info, p, group)
        a, b = mine[p], theirs[1 - p]
        lses, deltas = [], []
        for part in range(2):
            top, total = merge(
                (a[2 * part : 2 * part + 1], a[2 * part + 1 : 2 * part + 2]),
                (b[2 * part : 2 * part + 1], b[2 * part + 1 : 2 * part + 2]),
            )
            lses.append(top + jnp.log2(total))
            deltas.append(jnp.where(p == 0, a[4 + part : 5 + part], b[4 + part : 5 + part]))
        early_mask = mask_of(firsts[0], [k[0] for k in keys])
        late_mask = mask_of(firsts[1], [k[1] for k in keys])
        late = add(p, 1, 0, lses[1], deltas[1], None)
        late += add(p, 1, 1, lses[1], deltas[1], None)
        late += add(p, 1, 2, lses[1], deltas[1], late_mask)
        early = add(p, 0, 0, lses[0], deltas[0], early_mask)
        if last:
            late += dq_in[1, p]
            early += dq_in[0, p]
        dq[1, p] = late
        dq[0, p] = early
        dq[sel, p] += add(
            p,
            sel,
            sel_keys,
            jnp.where(sel == 1, lses[1], lses[0]),
            jnp.where(sel == 1, deltas[1], deltas[0]),
            None,
        )
        return carry

    lax.fori_loop(0, 2, step, 0)
    for side, out in enumerate((out_own, out_oth)):
        for b in range(4):
            rows = pl.ds(b * HALF, HALF)
            for j in range(4):
                cols = pl.ds(128 * j, 128)
                out[b, pl.ds(128 * j, HALF), :] = dk[side, rows, cols].astype(BF)
                out[b, pl.ds(128 * j + HALF, HALF), :] = dk[2 + side, rows, cols].astype(BF)
            out[b, 512:576, :] = jnp.concatenate(
                [dk[side, rows, 512:576], dk[2 + side, rows, 512:576]], axis=1
            ).astype(BF)
    if last:
        for part in range(2):
            dq_own[part] = dq[part, 0].T
            dq_send[part] = dq[part, 1].T.astype(BF)


def query_kernel(own, recv, w, q, nope, rope, dw):
    def total(part, rows, cols):
        return (own[part, rows, cols] + recv[part, rows, cols].astype(F32)).astype(BF)

    pairs = []
    for h in range(HEADS):
        rows = pl.ds(h * HALF, HALF)
        lat = jnp.concatenate([total(part, rows, slice(0, LAT)) for part in range(2)], axis=0)
        weights = w[pl.ds(h * NOPE, NOPE), :]
        nope[:, pl.ds(h * NOPE, NOPE)] = dot_nt(lat, weights).astype(BF)
        dw[pl.ds(h * NOPE, NOPE), :] = dot(q[:, pl.ds(h * NOPE, NOPE)].T, lat).astype(BF)
        pairs.append(
            jnp.concatenate([total(part, rows, slice(512, 640)) for part in range(2)], axis=0)
        )
    for k in range(HEADS // 2):
        rope[:, pl.ds(128 * k, 128)] = jnp.concatenate(
            [pairs[2 * k][:, :ROPE], pairs[2 * k + 1][:, :ROPE]], axis=1
        )


def shift(x, axis, steps):
    n = lax.axis_size(axis)
    return lax.ppermute(x, axis, [(i, (i + steps) % n) for i in range(n)])


def swap(x, axis):
    return shift(x, axis, 1)


def summed(*xs):
    total = xs[0].astype(F32)
    for x in xs[1:]:
        total = total + x.astype(F32)
    return total


def on_device(query_nope, query_rope, latent, rope_key, grad_out, saved_out, up_key):
    core, z, xl = lax.axis_index("core"), lax.axis_index("z"), lax.axis_index("xl")
    info = jnp.stack([core, z, xl]).astype(jnp.int32)
    (packed,) = call(pack_kernel, [((PACK, 128), BF)], 3)(latent, rope_key, up_key)
    column = {0: packed}
    up = down = packed
    for k in range(1, 4):
        up, down = shift(up, "z", 1), shift(down, "z", -1)
        column[8 - k], column[k] = up, down
    mid = PACK // 2
    column[4] = jnp.concatenate([shift(up[:mid], "z", 1), shift(down[mid:], "z", -1)], axis=0)
    across = {r: swap(column[r], "xl") for r in range(8)}
    packs = [side[r] for group in GROUPS for r in group for side in (column, across)]
    w_own = jnp.stack([x[576:] for x in packs])
    w_oth = swap(w_own, "core")
    g_oth = swap(grad_out, "core")
    qr_oth = swap(query_rope, "core")
    q_oth = swap(query_nope, "core")
    g_rows, qr_rows, delta = call(
        prep_kernel,
        [((2, 2, ROWS, LAT), BF), ((2, 2, ROWS, 128), BF), ((2, ROWS), F32)],
        5,
    )(grad_out, g_oth, query_rope, qr_oth, saved_out)
    kall, w_full, qf, stats = call(
        forward_kernel,
        [
            ((2, 4, 256, WIDE), BF),
            ((HEADS * NOPE, LAT), BF),
            ((2, 2, ROWS, WIDE), BF),
            ((2, 8, ROWS), F32),
        ],
        21,
        flops=3_000_000_000,
        smem=1,
    )(info, *packs, w_oth, query_nope, q_oth, qr_rows, delta)
    their_stats = swap(stats, "core")
    scratch = [pltpu.VMEM((4, WIDE, 256), BF), pltpu.VMEM((4, 256, WIDE), F32)]
    blocks = ((4, GRAD, 128), BF)
    grads = {}
    others = {}
    dq = None
    for gi, group in enumerate(GROUPS):
        last = gi == 1

        def kernel(*refs, group=group, last=last):
            backward_kernel(group, last, *refs)

        outs = [blocks, blocks]
        if last:
            outs += [((2, ROWS, WIDE), F32), ((2, ROWS, WIDE), BF)]
        else:
            outs += [((2, 2, WIDE, ROWS), F32)]
        own, oth, *rest = call(
            kernel,
            outs,
            5 + last,
            scratch + ([pltpu.VMEM((2, 2, WIDE, ROWS), F32)] if last else []),
            flops=9_000_000_000,
            smem=1,
        )(info, kall[gi], qf, g_rows, stats, their_stats, *([dq] if last else []))
        crossed = swap(oth, "xl")
        for b, r in enumerate(group):
            grads[r], others[r] = own[b], crossed[b]
        if last:
            dq_own, dq_send = rest
        else:
            (dq,) = rest
    dq_recv = swap(dq_send, "core")
    nope_grad, rope_grad, dw = call(
        query_kernel,
        [((128, HEADS * NOPE), BF), ((128, HEADS * ROPE), BF), ((HEADS * NOPE, LAT), BF)],
        4,
        flops=600_000_000,
    )(dq_own, dq_recv, w_full, query_nope)
    mid = GRAD // 2
    both = summed(grads[4], others[4]).astype(BF)
    up, down = shift(both[:mid], "z", 1), shift(both[mid:], "z", -1)
    fill = jnp.zeros((mid, 128), BF)
    up, down = jnp.concatenate([up, fill]), jnp.concatenate([fill, down])
    for k in (3, 2, 1):
        up = shift(summed(grads[k], others[k], up).astype(BF), "z", 1)
        down = shift(summed(grads[8 - k], others[8 - k], down).astype(BF), "z", -1)
    total = summed(grads[0], others[0], up, down)
    part = total.astype(BF)
    total = summed(total, *[shift(part, "y", k) for k in (1, 2, 3)])
    total = summed(total, swap(total.astype(BF), "xh"))
    lat_grad = jnp.concatenate([total[128 * j : 128 * j + 128] for j in range(4)], axis=1)
    rope_key_grad = jnp.concatenate([total[512:576, :ROPE], total[512:576, ROPE:]], axis=0)
    dw_parts = lax.all_to_all(
        dw.reshape(32, 32, LAT), ("xl", "z", "core"), split_axis=0, concat_axis=0, tiled=True
    )
    dw_total = jnp.sum(dw_parts.astype(F32), axis=0)
    return lat_grad, rope_key_grad, nope_grad, rope_grad, dw_total


def solution(mesh):
    fine = Mesh(mesh.devices.reshape(2, 4, 2, 8, 2), ("xh", "y", "xl", "z", "core"))
    dp, ctx = ("xh", "y"), ("xl", "z", "core")
    return jax.shard_map(
        on_device,
        mesh=fine,
        in_specs=(
            P(ctx, dp),
            P(ctx, dp),
            P(ctx, None),
            P(ctx, None),
            P(ctx, dp),
            P(ctx, dp),
            P(dp + ctx, None),
        ),
        out_specs=(P(ctx, None), P(ctx, None), P(ctx, dp), P(ctx, dp), P(dp + ctx, None)),
        check_vma=False,
    )
```

```python
import math

import jax
import jax.numpy as jnp
from jax import lax
from jax.experimental import pallas as pl
from jax.experimental.pallas import tpu as pltpu
from jax.sharding import Mesh
from jax.sharding import PartitionSpec as P

NOPE = 128
ROPE = 64
LAT = 512
HEADS = 8
HALF = 64
ROWS = HEADS * HALF
WIDE = 640
PACK = 704
GRAD = 576
SCALE = 1.0 / math.sqrt(NOPE + ROPE)
LOG2E = math.log2(math.e)
LOW = -1e30
BF = jnp.bfloat16
F32 = jnp.float32
GROUPS = ((4, 3, 5, 2), (6, 1, 7, 0))
PIECES = (
    ((0, 0), (1, 0), (0, 7), (0, 1)),
    ((0, 6), (0, 2), (1, 7), (1, 1)),
    ((0, 5), (0, 3), (1, 6), (1, 2)),
    ((0, 4), (1, 5), (1, 3)),
    ((1, 4),),
)
PLACES = {place: (i, j) for i, piece in enumerate(PIECES) for j, place in enumerate(piece)}
VMEM_LIMIT = 48 * 1024 * 1024


def dot(a, b):
    return lax.dot_general(a, b, (((1,), (0,)), ((), ())), preferred_element_type=F32)


def dot_nt(a, b):
    return lax.dot_general(a, b, (((1,), (1,)), ((), ())), preferred_element_type=F32)


def call(kernel, outs, count, scratch=(), flops=0, smem=0):
    vm = pl.BlockSpec(memory_space=pltpu.VMEM)
    sm = pl.BlockSpec(memory_space=pltpu.SMEM)
    return pl.pallas_call(
        kernel,
        out_shape=[jax.ShapeDtypeStruct(s, d) for s, d in outs],
        in_specs=[sm] * smem + [vm] * count,
        out_specs=[vm] * len(outs),
        scratch_shapes=list(scratch),
        compiler_params=pltpu.CompilerParams(vmem_limit_bytes=VMEM_LIMIT),
        cost_estimate=pl.CostEstimate(flops=flops, bytes_accessed=4_000_000, transcendentals=0),
    )


def pack_kernel(lat, rope, w, out):
    for j in range(4):
        cols = pl.ds(128 * j, 128)
        out[pl.ds(128 * j, 128), :] = lat[:, cols]
        out[pl.ds(576 + 32 * j, 32), :] = w[:, cols]
    out[512:576, :] = rope[...]


def rows_kernel(count, *refs):
    packs, outs = refs[:count], refs[count:]
    for i, pack in enumerate(packs):
        outs[0][pl.ds(128 * i, 128), :] = pack[576:704, :]
    if len(outs) > 1:
        outs[1][...] = packs[0][576:704, :]


def prep_kernel(g_own, g_oth, qr_own, qr_oth, o_own, g_out, qr_out, delta):
    for p, (g, qr) in enumerate(((g_own, qr_own), (g_oth, qr_oth))):
        for part in range(2):
            rows = pl.ds(part * HALF, HALF)
            for h in range(HEADS):
                g_out[part, p, pl.ds(h * HALF, HALF), :] = g[rows, pl.ds(h * LAT, LAT)]
            for k in range(HEADS // 2):
                pair = qr[rows, pl.ds(128 * k, 128)]
                zero = jnp.zeros((HALF, ROPE), BF)
                qr_out[part, p, pl.ds(2 * k * HALF, HALF), :] = jnp.concatenate(
                    [pair[:, :ROPE], zero], axis=1
                )
                qr_out[part, p, pl.ds((2 * k + 1) * HALF, HALF), :] = jnp.concatenate(
                    [pair[:, ROPE:], zero], axis=1
                )
    for part in range(2):
        rows = pl.ds(part * HALF, HALF)
        for k in range(HEADS // 2):
            halves = []
            for h in (2 * k, 2 * k + 1):
                cols = pl.ds(h * LAT, LAT)
                prod = g_own[rows, cols].astype(F32) * o_own[rows, cols].astype(F32)
                halves.append(
                    prod[:, 0:128] + prod[:, 128:256] + prod[:, 256:384] + prod[:, 384:512]
                )
            both = jnp.concatenate(halves, axis=0).T
            delta[pl.ds(part, 1), pl.ds(128 * k, 128)] = jnp.sum(both, axis=0, keepdims=True)


def positions_of(info, p, group):
    core, z, xl = info[0], info[1], info[2]
    owner = 2 * (xl * 8 + z) + jnp.where(p == 0, core, 1 - core)
    keys = []
    for r in group:
        e = 2 * (xl * 8 + ((z + r) & 7)) + core
        keys.append((e * HALF, (63 - e) * HALF))
    return (owner * HALF, (63 - owner) * HALF), keys


def mask_of(first_row, key_rows):
    key = lax.broadcasted_iota(jnp.int32, (HALF, ROWS), 0)
    tok = lax.broadcasted_iota(jnp.int32, (HALF, ROWS), 1) & (HALF - 1)
    diff = key - tok
    return jnp.concatenate([diff <= first_row - k for k in key_rows], axis=0)


def stats_of(s):
    top = jnp.max(s, axis=0, keepdims=True)
    return top, jnp.sum(jnp.exp2(s - top), axis=0, keepdims=True)


def merge(a, b):
    top = jnp.maximum(a[0], b[0])
    return top, a[1] * jnp.exp2(a[0] - top) + b[1] * jnp.exp2(b[0] - top)


def forward_kernel(info, *refs):
    packs, refs = refs[:16], refs[16:]
    pieces, refs = refs[: len(PIECES)], refs[len(PIECES) :]
    (q_own, q_oth, qr, delta, *kalls, w_full, qf, stats) = refs
    core, z, xl = info[0], info[1], info[2]
    for gi, group in enumerate(GROUPS):
        kall = kalls[gi]
        for b, r in enumerate(group):
            for side in range(2):
                pack = packs[(gi * 4 + b) * 2 + side]
                rows = pl.ds(b * HALF, HALF)
                for j in range(4):
                    cols = pl.ds(128 * j, 128)
                    kall[side, rows, cols] = pack[pl.ds(128 * j, HALF), :]
                    kall[2 + side, rows, cols] = pack[pl.ds(128 * j + HALF, HALF), :]
                ropes = jnp.concatenate(
                    [pack[512:576, :].T, jnp.zeros((2 * HALF, 128 - ROPE), BF)], axis=1
                )
                kall[side, rows, 512:640] = ropes[:HALF]
                kall[2 + side, rows, 512:640] = ropes[HALF:]
                column = xl if side == 0 else 1 - xl
                chip = column * 8 + ((z + r) & 7)
                piece, at = PLACES[(side, r)]
                own_row = pl.multiple_of((2 * chip + core) * 32, 32)
                oth_row = pl.multiple_of((2 * chip + 1 - core) * 32, 32)
                for j in range(4):
                    cols = pl.ds(128 * j, 128)
                    w_full[pl.ds(own_row, 32), cols] = pack[pl.ds(576 + 32 * j, 32), :]
                    w_full[pl.ds(oth_row, 32), cols] = pieces[piece][
                        pl.ds(128 * at + 32 * j, 32), :
                    ]
    for p, q in enumerate((q_own, q_oth)):
        for h in range(HEADS):
            lat = dot(q[:, pl.ds(h * NOPE, NOPE)], w_full[pl.ds(h * NOPE, NOPE), :]).astype(BF)
            qf[0, p, pl.ds(h * HALF, HALF), 0:512] = lat[:HALF]
            qf[1, p, pl.ds(h * HALF, HALF), 0:512] = lat[HALF:]
        for part in range(2):
            qf[part, p, :, 512:640] = qr[part, p]
    sel = 1 - xl
    sel_keys = jnp.where(xl == 0, 3, 1)
    factor = SCALE * LOG2E

    def step(p, carry):
        late = early = cross = None
        for gi, group in enumerate(GROUPS):
            firsts, keys = positions_of(info, p, group)
            for i in range(3):
                s = dot_nt(kalls[gi][i], qf[1, p]) * factor
                if i == 2:
                    s = jnp.where(mask_of(firsts[1], [k[1] for k in keys]), s, LOW)
                now = stats_of(s)
                late = now if late is None else merge(late, now)
            s = dot_nt(kalls[gi][0], qf[0, p]) * factor
            now = stats_of(jnp.where(mask_of(firsts[0], [k[0] for k in keys]), s, LOW))
            early = now if early is None else merge(early, now)
            now = stats_of(dot_nt(kalls[gi][sel_keys], qf[sel, p]) * factor)
            cross = now if cross is None else merge(cross, now)
        more_late, more_early = merge(late, cross), merge(early, cross)
        late = [jnp.where(sel == 1, a, b) for a, b in zip(more_late, late)]
        early = [jnp.where(sel == 0, a, b) for a, b in zip(more_early, early)]
        zero = jnp.zeros((2, ROWS), F32)
        stats[p] = jnp.concatenate([*early, *late, delta[...], zero], axis=0)
        return carry

    lax.fori_loop(0, 2, step, 0)


def backward_kernel(group, last, info, kall, qf, g, mine, theirs, *refs):
    if last:
        dq_in, *outs, dq_own, dq_send, kt, dk, dq = refs
    else:
        *outs, dq, kt, dk = refs
    xl = info[2]
    sel = 1 - xl
    sel_keys = jnp.where(xl == 0, 3, 1)
    factor = SCALE * LOG2E
    for i in range(4):
        kt[i] = kall[i].T
    dk[...] = jnp.zeros_like(dk)

    def parts(p, part, keys, lse, delta, mask):
        queries, grads = qf[part, p], g[part, p]
        prob = jnp.exp2(dot_nt(keys, queries) * factor - lse)
        if mask is not None:
            rows = keys.shape[0] - mask.shape[0]
            tail = jnp.where(mask, prob[rows:], 0.0)
            prob = jnp.concatenate([prob[:rows], tail], axis=0) if rows else tail
        dprob = dot_nt(keys[:, :LAT], grads)
        ds = ((prob * SCALE) * (dprob - delta)).astype(BF)
        return ds, dot(ds, queries), dot(prob.astype(BF), grads)

    for p in range(2):
        firsts, keys = positions_of(info, p, group)
        a, b = mine[p], theirs[1 - p]
        lses, deltas = [], []
        for part in range(2):
            top, total = merge(
                (a[2 * part : 2 * part + 1], a[2 * part + 1 : 2 * part + 2]),
                (b[2 * part : 2 * part + 1], b[2 * part + 1 : 2 * part + 2]),
            )
            lses.append(top + jnp.log2(total))
            deltas.append((a if p == 0 else b)[4 + part : 5 + part])
        early_mask = mask_of(firsts[0], [k[0] for k in keys])
        late_mask = mask_of(firsts[1], [k[1] for k in keys])
        ds, full, lat = parts(
            p, 1, kall[0:3].reshape(768, WIDE), lses[1], deltas[1], late_mask
        )
        late = None
        for i in range(3):
            rows = slice(256 * i, 256 * i + 256)
            dk[i, :, 0:LAT] += full[rows, :LAT] + lat[rows]
            dk[i, :, LAT:] += full[rows, LAT:]
            term = dot(kt[i], ds[rows])
            late = term if late is None else late + term
        ds, full, lat = parts(p, 0, kall[0], lses[0], deltas[0], early_mask)
        dk[0, :, 0:LAT] += full[:, :LAT] + lat
        dk[0, :, LAT:] += full[:, LAT:]
        early = dot(kt[0], ds)
        if last:
            late += dq_in[1, p]
            early += dq_in[0, p]
        dq[1, p] = late
        dq[0, p] = early
        lse = jnp.where(sel == 1, lses[1], lses[0])
        delta = jnp.where(sel == 1, deltas[1], deltas[0])
        ds, full, lat = parts(p, sel, kall[sel_keys], lse, delta, None)
        dk[sel_keys, :, 0:LAT] += full[:, :LAT] + lat
        dk[sel_keys, :, LAT:] += full[:, LAT:]
        dq[sel, p] += dot(kt[sel_keys], ds)

    for side in range(2):
        for b in range(4):
            out = outs[side * 4 + b]
            rows = pl.ds(b * HALF, HALF)
            for j in range(4):
                cols = pl.ds(128 * j, 128)
                out[pl.ds(128 * j, HALF), :] = dk[side, rows, cols].astype(BF)
                out[pl.ds(128 * j + HALF, HALF), :] = dk[2 + side, rows, cols].astype(BF)
            ropes = jnp.concatenate([dk[side, rows, 512:640], dk[2 + side, rows, 512:640]], axis=0)
            out[512:576, :] = ropes.T[:ROPE].astype(BF)
    if last:
        for part in range(2):
            dq_own[part] = dq[part, 0].T
            dq_send[part] = dq[part, 1].T.astype(BF)


def query_kernel(info, own, recv, w, q, nope, rope, dw_own, dw_oth, dw):
    def total(part, rows, cols):
        return (own[part, rows, cols] + recv[part, rows, cols].astype(F32)).astype(BF)

    pairs = []
    for h in range(HEADS):
        rows = pl.ds(h * HALF, HALF)
        lat = jnp.concatenate([total(part, rows, slice(0, LAT)) for part in range(2)], axis=0)
        weights = w[pl.ds(h * NOPE, NOPE), :]
        nope[:, pl.ds(h * NOPE, NOPE)] = dot_nt(lat, weights).astype(BF)
        dw[pl.ds(h * NOPE, NOPE), :] = dot(q[:, pl.ds(h * NOPE, NOPE)].T, lat).astype(BF)
        pairs.append(
            jnp.concatenate([total(part, rows, slice(512, 640)) for part in range(2)], axis=0)
        )
    for k in range(HEADS // 2):
        rope[:, pl.ds(128 * k, 128)] = jnp.concatenate(
            [pairs[2 * k][:, :ROPE], pairs[2 * k + 1][:, :ROPE]], axis=1
        )
    core, z, xl = info[0], info[1], info[2]
    for side in range(2):
        for r in range(8):
            chip = (xl if side == 0 else 1 - xl) * 8 + ((z + r) & 7)
            for out, parity in ((dw_own, core), (dw_oth, 1 - core)):
                out[side, r] = dw[pl.ds(pl.multiple_of((2 * chip + parity) * 32, 32), 32), :]


def shift(x, axis, steps):
    n = lax.axis_size(axis)
    return lax.ppermute(x, axis, [(i, (i + steps) % n) for i in range(n)])


def swap(x, axis):
    return shift(x, axis, 1)


def summed(*xs):
    total = xs[0].astype(F32)
    for x in xs[1:]:
        total = total + x.astype(F32)
    return total


def fence(*xs):
    return lax.optimization_barrier(xs)


def up_rows(*packs, alone=False):
    outs = [((128 * len(packs), 128), BF)] + ([((128, 128), BF)] if alone else [])

    def kernel(*refs):
        rows_kernel(len(packs), *refs)

    return call(kernel, outs, len(packs))(*packs)


def on_device(query_nope, query_rope, latent, rope_key, grad_out, saved_out, up_key):
    core, z, xl = lax.axis_index("core"), lax.axis_index("z"), lax.axis_index("xl")
    info = jnp.stack([core, z, xl]).astype(jnp.int32)
    (packed,) = call(pack_kernel, [((PACK, 128), BF)], 3)(latent, rope_key.T, up_key)
    packed, grad_out, query_rope, query_nope = fence(packed, grad_out, query_rope, query_nope)
    u1, d1, x0 = shift(packed, "z", 1), shift(packed, "z", -1), swap(packed, "xl")
    qr_oth, q_oth, g_oth = (swap(x, "core") for x in (query_rope, query_nope, grad_out))
    u1, d1, x0, qr_oth, q_oth, g_oth = fence(u1, d1, x0, qr_oth, q_oth, g_oth)
    u2, d2, xu1, xd1 = shift(u1, "z", 1), shift(d1, "z", -1), swap(u1, "xl"), swap(d1, "xl")
    w0 = swap(up_rows(packed, x0, u1, d1)[0], "core")
    g_rows, qr_rows, delta = call(
        prep_kernel,
        [((2, 2, ROWS, LAT), BF), ((2, 2, ROWS, 128), BF), ((2, ROWS), F32)],
        5,
    )(grad_out, g_oth, query_rope, qr_oth, saved_out)
    u2, d2, xu1, xd1, w0, g_rows = fence(u2, d2, xu1, xd1, w0, g_rows)
    u3, d3, xu2, xd2 = shift(u2, "z", 1), shift(d2, "z", -1), swap(u2, "xl"), swap(d2, "xl")
    w1 = swap(up_rows(u2, d2, xu1, xd1)[0], "core")
    u3, d3, xu2, xd2, w1 = fence(u3, d3, xu2, xd2, w1)
    u4, xu3, xd3 = shift(u3, "z", 1), swap(u3, "xl"), swap(d3, "xl")
    w2 = swap(up_rows(u3, d3, xu2, xd2)[0], "core")
    u4, xu3, xd3, w2 = fence(u4, xu3, xd3, w2)
    x4 = swap(u4, "xl")
    w3, w4 = up_rows(u4, xu3, xd3, alone=True)
    w3 = swap(w3, "core")
    w4 = lax.ppermute(w4, ("xl", "core"), [(i, 3 - i) for i in range(4)])
    column = {0: packed, 7: u1, 1: d1, 6: u2, 2: d2, 5: u3, 3: d3, 4: u4}
    across = {0: x0, 7: xu1, 1: xd1, 6: xu2, 2: xd2, 5: xu3, 3: xd3, 4: x4}
    packs = [side[r] for group in GROUPS for r in group for side in (column, across)]
    *kalls, w_full, qf, stats = call(
        forward_kernel,
        [
            ((4, 256, WIDE), BF),
            ((4, 256, WIDE), BF),
            ((HEADS * NOPE, LAT), BF),
            ((2, 2, ROWS, WIDE), BF),
            ((2, 8, ROWS), F32),
        ],
        25,
        flops=3_000_000_000,
        smem=1,
    )(info, *packs, w0, w1, w2, w3, w4, query_nope, q_oth, qr_rows, delta)
    their_stats = swap(stats, "core")
    scratch = [pltpu.VMEM((4, WIDE, 256), BF), pltpu.VMEM((4, 256, WIDE), F32)]
    blocks = [((GRAD, 128), BF)] * 8

    def backward(gi, last, *more):
        def kernel(*refs):
            backward_kernel(GROUPS[gi], last, *refs)

        outs = [((2, ROWS, WIDE), F32), ((2, ROWS, WIDE), BF)]
        if not last:
            outs = [((2, 2, WIDE, ROWS), F32)]
        results = call(
            kernel,
            blocks + outs,
            5 + last,
            scratch + ([pltpu.VMEM((2, 2, WIDE, ROWS), F32)] if last else []),
            flops=9_000_000_000,
            smem=1,
        )(info, kalls[gi], qf, g_rows, stats, their_stats, *more)
        own, oth, rest = results[:4], results[4:8], results[8:]
        return dict(zip(GROUPS[gi], own)), dict(zip(GROUPS[gi], oth)), rest

    own, oth, (dq,) = backward(0, False)
    first = dict(zip(GROUPS[0], fence(*[oth[r] for r in GROUPS[0]])))
    cross = {r: swap(first[r], "xl") for r in GROUPS[0]}
    own2, oth2, (dq_own, dq_send) = backward(1, True, dq)
    own.update(own2)
    c4, c3, c5, c2, dq_send, o6, o1, o7, o0 = fence(
        cross[4], cross[3], cross[5], cross[2], dq_send, *[oth2[r] for r in GROUPS[1]]
    )
    mid = GRAD // 2
    both = summed(own[4], c4).astype(BF)
    up, down = shift(both[:mid], "z", 1), shift(both[mid:], "z", -1)
    dq_recv = swap(dq_send, "core")
    c6, c1 = swap(o6, "xl"), swap(o1, "xl")
    nope_grad, rope_grad, dw_own, dw_oth = call(
        query_kernel,
        [
            ((128, HEADS * NOPE), BF),
            ((128, HEADS * ROPE), BF),
            ((2, 8, 32, LAT), BF),
            ((2, 8, 32, LAT), BF),
        ],
        4,
        [pltpu.VMEM((HEADS * NOPE, LAT), BF)],
        flops=600_000_000,
        smem=1,
    )(info, dq_own, dq_recv, w_full, query_nope)
    up, down, c6, c1, dw_oth = fence(up, down, c6, c1, dw_oth)
    fill = jnp.zeros((mid, 128), BF)
    up = shift(summed(own[3], c3, jnp.concatenate([up, fill])).astype(BF), "z", 1)
    down = shift(summed(own[5], c5, jnp.concatenate([fill, down])).astype(BF), "z", -1)
    c7, c0 = swap(o7, "xl"), swap(o0, "xl")
    dw_recv = swap(dw_oth, "core")
    up, down, c7, c0, dw_recv = fence(up, down, c7, c0, dw_recv)
    up = shift(summed(own[2], c2, up).astype(BF), "z", 1)
    down = shift(summed(own[6], c6, down).astype(BF), "z", -1)
    dw_sum = summed(dw_own, dw_recv)
    dw_recv = swap(dw_sum[1].astype(BF), "xl")
    up, down, dw_recv = fence(up, down, dw_recv)
    up = shift(summed(own[1], c1, up).astype(BF), "z", 1)
    down = shift(summed(own[7], c7, down).astype(BF), "z", -1)
    dw_sum = summed(dw_sum[0], dw_recv)
    ahead, behind = shift(dw_sum[3:5].astype(BF), "z", 2), shift(dw_sum[5].astype(BF), "z", -2)
    up, down, ahead, behind = fence(up, down, ahead, behind)
    total = summed(own[0], c0, up, down)
    part = total.astype(BF)
    sides = [shift(part, "y", k) for k in (1, 2, 3)]
    dw_parts = [
        shift(summed(dw_sum[1], ahead[0]).astype(BF), "z", 1),
        shift(summed(dw_sum[2], ahead[1]).astype(BF), "z", 2),
        shift(summed(dw_sum[7], behind).astype(BF), "z", -1),
        shift(dw_sum[6].astype(BF), "z", -2),
    ]
    *sides, d1, d2, d3, d4 = fence(*sides, *dw_parts)
    total = summed(total, *sides)
    total = summed(total, swap(total.astype(BF), "xh"))
    dw_total = summed(dw_sum[0], d1, d2, d3, d4)
    lat_grad = jnp.concatenate([total[128 * j : 128 * j + 128] for j in range(4)], axis=1)
    return lat_grad, total[512:576].T, nope_grad, rope_grad, dw_total


def solution(mesh):
    fine = Mesh(mesh.devices.reshape(2, 4, 2, 8, 2), ("xh", "y", "xl", "z", "core"))
    dp, ctx = ("xh", "y"), ("xl", "z", "core")
    return jax.shard_map(
        on_device,
        mesh=fine,
        in_specs=(
            P(ctx, dp),
            P(ctx, dp),
            P(ctx, None),
            P(ctx, None),
            P(ctx, dp),
            P(ctx, dp),
            P(dp + ctx, None),
        ),
        out_specs=(P(ctx, None), P(ctx, None), P(ctx, dp), P(ctx, dp), P(dp + ctx, None)),
        check_vma=False,
    )
```

```python
import math

import jax
import jax.numpy as jnp
from jax import lax
from jax.experimental import pallas as pl
from jax.experimental.pallas import tpu as pltpu
from jax.sharding import Mesh
from jax.sharding import PartitionSpec as P

NOPE = 128
ROPE = 64
LAT = 512
HEADS = 8
HALF = 64
ROWS = HEADS * HALF
WIDE = 640
PACK = 576
SCALE = 1.0 / math.sqrt(NOPE + ROPE)
LOG2E = math.log2(math.e)
LOW = -1e30
BF = jnp.bfloat16
F32 = jnp.float32
FAR, NEAR = (4, 3, 5), (2, 6, 1, 7, 0)
OFFSETS = FAR + NEAR
KEYS = len(OFFSETS) * HALF
MEGA = 1024 * 1024


def dot(a, b):
    return lax.dot_general(a, b, (((1,), (0,)), ((), ())), preferred_element_type=F32)


def dot_nt(a, b):
    return lax.dot_general(a, b, (((1,), (1,)), ((), ())), preferred_element_type=F32)


def call(kernel, outs, count, scratch=(), flops=0, smem=0, mega=6, space=pltpu.VMEM):
    vm = pl.BlockSpec(memory_space=pltpu.VMEM)
    sm = pl.BlockSpec(memory_space=pltpu.SMEM)
    return pl.pallas_call(
        kernel,
        out_shape=[jax.ShapeDtypeStruct(s, d) for s, d in outs],
        in_specs=[sm] * smem + [pl.BlockSpec(memory_space=space)] * count,
        out_specs=[vm] * len(outs),
        scratch_shapes=list(scratch),
        compiler_params=pltpu.CompilerParams(vmem_limit_bytes=mega * MEGA),
        cost_estimate=pl.CostEstimate(flops=flops, bytes_accessed=1_000, transcendentals=0),
    )


def pack_kernel(lat, rope, w, out, sems):
    copies = [pltpu.make_async_copy(rope, out.at[512:576], sems.at[8])]
    for j in range(4):
        part, rows = pl.ds(128 * j, 128), pl.ds(PACK + 32 * j, 32)
        copies.append(pltpu.make_async_copy(lat.at[:, part], out.at[part], sems.at[j]))
        copies.append(pltpu.make_async_copy(w.at[:, part], out.at[rows], sems.at[4 + j]))
    for copy in copies:
        copy.start()
    for copy in copies:
        copy.wait()


def unpack_kernel(*refs):
    packs, (early, late, w) = refs[:-3], refs[-3:]
    for b, pack in enumerate(packs):
        rows = pl.ds(b * HALF, HALF)
        for j in range(4):
            cols = pl.ds(128 * j, 128)
            early[rows, cols] = pack[pl.ds(128 * j, HALF), :]
            late[rows, cols] = pack[pl.ds(128 * j + HALF, HALF), :]
            w[b, :, cols] = pack[pl.ds(PACK + 32 * j, 32), :]
        ropes = jnp.concatenate(
            [pack[512:576, :].T, jnp.zeros((2 * HALF, 128 - ROPE), BF)], axis=1
        )
        early[rows, 512:640] = ropes[:HALF]
        late[rows, 512:640] = ropes[HALF:]


def prep_kernel(g_own, g_oth, qr_own, qr_oth, o_own, g_out, qr_out, delta):
    for p, (g, qr) in enumerate(((g_own, qr_own), (g_oth, qr_oth))):
        for part in range(2):
            rows = pl.ds(part * HALF, HALF)
            for h in range(HEADS):
                g_out[part, p, pl.ds(h * HALF, HALF), :] = g[rows, pl.ds(h * LAT, LAT)]
            for k in range(HEADS // 2):
                pair = qr[rows, pl.ds(128 * k, 128)]
                zero = jnp.zeros((HALF, ROPE), BF)
                qr_out[part, p, pl.ds(2 * k * HALF, HALF), :] = jnp.concatenate(
                    [pair[:, :ROPE], zero], axis=1
                )
                qr_out[part, p, pl.ds((2 * k + 1) * HALF, HALF), :] = jnp.concatenate(
                    [pair[:, ROPE:], zero], axis=1
                )
    for part in range(2):
        rows = pl.ds(part * HALF, HALF)
        for k in range(HEADS // 2):
            halves = []
            for h in (2 * k, 2 * k + 1):
                cols = pl.ds(h * LAT, LAT)
                prod = g_own[rows, cols].astype(F32) * o_own[rows, cols].astype(F32)
                halves.append(
                    prod[:, 0:128] + prod[:, 128:256] + prod[:, 256:384] + prod[:, 384:512]
                )
            both = jnp.concatenate(halves, axis=0).T
            delta[pl.ds(part, 1), pl.ds(128 * k, 128)] = jnp.sum(both, axis=0, keepdims=True)


def positions_of(info, p):
    core, z, xl = info[0], info[1], info[2]
    owner = 2 * (xl * 8 + z) + jnp.where(p == 0, core, 1 - core)
    early, late = [], []
    for r in OFFSETS:
        e = 2 * (xl * 8 + ((z + r) & 7)) + core
        early.append(e * HALF)
        late.append((63 - e) * HALF)
    return owner * HALF, (63 - owner) * HALF, early, late


def mask_of(first_row, key_rows):
    key = lax.broadcasted_iota(jnp.int32, (HALF, ROWS), 0)
    tok = lax.broadcasted_iota(jnp.int32, (HALF, ROWS), 1) & (HALF - 1)
    diff = key - tok
    return jnp.concatenate([diff <= first_row - k for k in key_rows], axis=0)


def stats_of(s):
    top = jnp.max(s, axis=0, keepdims=True)
    return top, jnp.sum(jnp.exp2(s - top), axis=0, keepdims=True)


def merge(a, b):
    top = jnp.maximum(a[0], b[0])
    return top, a[1] * jnp.exp2(a[0] - top) + b[1] * jnp.exp2(b[0] - top)


def latent_kernel(info, *refs):
    pieces, (q_own, q_oth, qr, w_full, qf) = refs[:8], refs[8:]
    core, z, xl = info[0], info[1], info[2]
    for i, (far, near) in enumerate(zip(pieces[0::2], pieces[1::2])):
        parity = core if i < 2 else 1 - core
        column = xl if i % 2 == 0 else 1 - xl
        for b, r in enumerate(OFFSETS):
            chip = column * 8 + ((z + r) & 7)
            at = pl.multiple_of((2 * chip + parity) * 32, 32)
            w_full[pl.ds(at, 32), :] = far[b] if b < len(FAR) else near[b - len(FAR)]
    for p, q in enumerate((q_own, q_oth)):
        for h in range(HEADS):
            lat = dot(q[:, pl.ds(h * NOPE, NOPE)], w_full[pl.ds(h * NOPE, NOPE), :]).astype(BF)
            qf[0, p, pl.ds(h * HALF, HALF), 0:512] = lat[:HALF]
            qf[1, p, pl.ds(h * HALF, HALF), 0:512] = lat[HALF:]
        for part in range(2):
            qf[part, p, :, 512:640] = qr[part, p]


def join_keys(parts, keys):
    count = len(FAR) * HALF
    for half in range(2):
        keys[half, 0:count, :] = parts[2 * half][...]
        keys[half, count:KEYS, :] = parts[2 * half + 1][...]


def own_stats_kernel(info, *refs):
    parts, (qf, keys, stats) = refs[:4], refs[4:]
    join_keys(parts, keys)
    factor = SCALE * LOG2E
    for p in range(2):
        first_early, first_late, early, late = positions_of(info, p)
        s = dot_nt(keys[0], qf[0, p]) * factor
        early_stats = stats_of(jnp.where(mask_of(first_early, early), s, LOW))
        s = dot_nt(keys[1], qf[1, p]) * factor
        late_stats = merge(
            stats_of(jnp.where(mask_of(first_late, late), s, LOW)),
            stats_of(dot_nt(keys[0], qf[1, p]) * factor),
        )
        stats[p] = jnp.concatenate([*early_stats, *late_stats], axis=0)


def all_stats_kernel(info, *refs):
    parts, (qf, own, delta, keys, stats) = refs[:4], refs[4:]
    join_keys(parts, keys)
    sel = 1 - info[2]
    factor = SCALE * LOG2E
    for p in range(2):
        cross = stats_of(dot_nt(keys[sel], qf[sel, p]) * factor)
        late = merge(
            (own[p, 2:3], own[p, 3:4]), stats_of(dot_nt(keys[0], qf[1, p]) * factor)
        )
        early = (own[p, 0:1], own[p, 1:2])
        more_late, more_early = merge(late, cross), merge(early, cross)
        late = [jnp.where(sel == 1, a, b) for a, b in zip(more_late, late)]
        early = [jnp.where(sel == 0, a, b) for a, b in zip(more_early, early)]
        zero = jnp.zeros((2, ROWS), F32)
        stats[p] = jnp.concatenate([*early, *late, delta[...], zero], axis=0)


def row_terms(mine, theirs, p):
    a, b = mine[p], theirs[1 - p]
    lses, deltas = [], []
    for part in range(2):
        top, total = merge(
            (a[2 * part : 2 * part + 1], a[2 * part + 1 : 2 * part + 2]),
            (b[2 * part : 2 * part + 1], b[2 * part + 1 : 2 * part + 2]),
        )
        lses.append(top + jnp.log2(total))
        deltas.append((a if p == 0 else b)[4 + part : 5 + part])
    return lses, deltas


def block_grads(keys, queries, grads, lse, delta, mask):
    prob = jnp.exp2(dot_nt(keys, queries) * (SCALE * LOG2E) - lse)
    if mask is not None:
        rows = keys.shape[0] - mask.shape[0]
        tail = jnp.where(mask, prob[rows:], 0.0)
        prob = jnp.concatenate([prob[:rows], tail], axis=0) if rows else tail
    dprob = dot_nt(keys[:, :LAT], grads)
    ds = ((prob * SCALE) * (dprob - delta)).astype(BF)
    return ds, dot(ds, queries), dot(prob.astype(BF), grads)


def add_grads(dk, at, full, lat):
    dk[at, :, 0:LAT] += full[:, :LAT] + lat
    dk[at, :, LAT:] += full[:, LAT:]


def put_grads(dk, b, out):
    rows = pl.ds(b * HALF, HALF)
    for j in range(4):
        cols = pl.ds(128 * j, 128)
        out[pl.ds(128 * j, HALF), :] = dk[0, rows, cols].astype(BF)
        out[pl.ds(128 * j + HALF, HALF), :] = dk[1, rows, cols].astype(BF)
    ropes = jnp.concatenate([dk[0, rows, 512:640], dk[1, rows, 512:640]], axis=0)
    out[512:576, :] = ropes.T[:ROPE].astype(BF)


def across_kernel(info, keys, qf, g, mine, theirs, far, near, last, dq, kt, dk):
    sel = 1 - info[2]
    for i in range(2):
        kt[i] = keys[i].T
    dk[...] = jnp.zeros_like(dk)
    for p in range(2):
        lses, deltas = row_terms(mine, theirs, p)
        ds, full, lat = block_grads(keys[0], qf[1, p], g[1, p], lses[1], deltas[1], None)
        add_grads(dk, 0, full, lat)
        late = dot(kt[0], ds)
        lse = jnp.where(sel == 1, lses[1], lses[0])
        delta = jnp.where(sel == 1, deltas[1], deltas[0])
        ds, full, lat = block_grads(keys[sel], qf[sel, p], g[sel, p], lse, delta, None)
        add_grads(dk, sel, full, lat)
        more = dot(kt[sel], ds)
        dq[1, p] = jnp.where(sel == 1, late + more, late).astype(BF)
        dq[0, p] = jnp.where(sel == 0, more, 0.0).astype(BF)
    for b in range(8):
        put_grads(dk, b, (far, near, last)[b // 3].at[b % 3])


def own_kernel(info, keys, qf, g, mine, theirs, dq, out, dq_own, dq_send, kt, dk):
    for i in range(2):
        kt[i] = keys[i].T
    dk[...] = jnp.zeros_like(dk)
    for p in range(2):
        first_early, first_late, early_keys, late_keys = positions_of(info, p)
        lses, deltas = row_terms(mine, theirs, p)
        ds, full, lat = block_grads(
            keys[...].reshape(2 * KEYS, WIDE),
            qf[1, p],
            g[1, p],
            lses[1],
            deltas[1],
            mask_of(first_late, late_keys),
        )
        add_grads(dk, 0, full[:KEYS], lat[:KEYS])
        add_grads(dk, 1, full[KEYS:], lat[KEYS:])
        late = dq[1, p] + dot(kt[0], ds[:KEYS]) + dot(kt[1], ds[KEYS:])
        ds, full, lat = block_grads(
            keys[0], qf[0, p], g[0, p], lses[0], deltas[0], mask_of(first_early, early_keys)
        )
        add_grads(dk, 0, full, lat)
        early = dq[0, p] + dot(kt[0], ds)
        for part, value in enumerate((early, late)):
            if p == 0:
                dq_own[part] = value.T.astype(BF)
            else:
                dq_send[part] = value.T.astype(BF)
    for b in range(8):
        put_grads(dk, b, out.at[b])


def query_kernel(info, own, recv, w, q, nope, rope, dw_own, dw_oth, dw):
    def total(part, rows, cols):
        return (own[part, rows, cols].astype(F32) + recv[part, rows, cols].astype(F32)).astype(BF)

    pairs = []
    for h in range(HEADS):
        rows = pl.ds(h * HALF, HALF)
        lat = jnp.concatenate([total(part, rows, slice(0, LAT)) for part in range(2)], axis=0)
        weights = w[pl.ds(h * NOPE, NOPE), :]
        nope[:, pl.ds(h * NOPE, NOPE)] = dot_nt(lat, weights).astype(BF)
        dw[pl.ds(h * NOPE, NOPE), :] = dot(q[:, pl.ds(h * NOPE, NOPE)].T, lat).astype(BF)
        pairs.append(
            jnp.concatenate([total(part, rows, slice(512, 640)) for part in range(2)], axis=0)
        )
    for k in range(HEADS // 2):
        rope[:, pl.ds(128 * k, 128)] = jnp.concatenate(
            [pairs[2 * k][:, :ROPE], pairs[2 * k + 1][:, :ROPE]], axis=1
        )
    core, xl = info[0], info[2]
    for side in range(2):
        for z in range(8):
            chip = (xl if side == 0 else 1 - xl) * 8 + z
            for out, parity in ((dw_own, core), (dw_oth, 1 - core)):
                out[side, z] = dw[pl.ds(pl.multiple_of((2 * chip + parity) * 32, 32), 32), :]


def shift(x, axis, steps):
    n = lax.axis_size(axis)
    return lax.ppermute(x, axis, [(i, (i + steps) % n) for i in range(n)])


def swap(x, axis):
    return shift(x, axis, 1)


def summed(*xs):
    total = xs[0].astype(F32)
    for x in xs[1:]:
        total = total + x.astype(F32)
    return total


def fence(*xs):
    return lax.optimization_barrier(xs)


def joined(grads, dw):
    return jnp.concatenate([grads, dw.reshape(-1, 128)], axis=0).astype(BF)


def shift_x(x, steps):
    return lax.ppermute(x, ("xh", "xl"), [(i, (i + steps) % 4) for i in range(4)])


def on_device(query_nope, query_rope, latent, rope_key, grad_out, saved_out, up_key):
    core, z, xl = lax.axis_index("core"), lax.axis_index("z"), lax.axis_index("xl")
    info = jnp.stack([core, z, xl]).astype(jnp.int32)
    (packed,) = call(
        pack_kernel,
        [((PACK + 128, 128), BF)],
        3,
        [pltpu.SemaphoreType.DMA((9,))],
        mega=2,
        space=pl.ANY,
    )(latent, rope_key.T, up_key)

    def unpack(*packs):
        n = len(packs)
        rows = ((n * HALF, WIDE), BF)
        return call(unpack_kernel, [rows, rows, ((n, 32, LAT), BF)], n)(*packs)

    packed, grad_out, query_rope, query_nope = fence(packed, grad_out, query_rope, query_nope)
    u1, d1 = shift(packed, "z", 1), shift(packed, "z", -1)
    qr_oth, g_oth = swap(query_rope, "core"), swap(grad_out, "core")
    u1, d1, qr_oth, g_oth, query_nope = fence(u1, d1, qr_oth, g_oth, query_nope)
    u2, d2 = shift(u1, "z", 1), shift(d1, "z", -1)
    g_rows, qr_rows, delta = call(
        prep_kernel,
        [((2, 2, ROWS, LAT), BF), ((2, 2, ROWS, 128), BF), ((2, ROWS), F32)],
        5,
    )(grad_out, g_oth, query_rope, qr_oth, saved_out)
    u2, d2, g_rows, qr_rows, query_nope = fence(u2, d2, g_rows, qr_rows, query_nope)
    u3, d3 = shift(u2, "z", 1), shift(d2, "z", -1)
    q_oth = swap(query_nope, "core")
    early_near, late_near, w_near = unpack(*fence(d2, u2, d1, u1, packed, q_oth)[:5])
    x_early_near, x_late_near = shift_x(early_near, 1), shift_x(late_near, -1)
    wx_near, wo_near = swap(w_near, "xl"), swap(w_near, "core")
    u3, d3 = fence(u3, d3)
    u4 = shift(u3, "z", 1)
    u4, x_early_near, x_late_near = fence(u4, x_early_near, x_late_near)
    early_far, late_far, w_far = unpack(u4, d3, u3)
    wxo_near = swap(wx_near, "core")
    wx_far, wo_far = swap(w_far, "xl"), swap(w_far, "core")
    wxo_far = lax.ppermute(w_far, ("xl", "core"), [(i, 3 - i) for i in range(4)])
    x_early_far, x_late_far = shift_x(early_far, 1), shift_x(late_far, -1)
    w_full, qf = call(
        latent_kernel,
        [((HEADS * NOPE, LAT), BF), ((2, 2, ROWS, WIDE), BF)],
        11,
        smem=1,
    )(
        info,
        *(w_far, w_near, wx_far, wx_near, wo_far, wo_near, wxo_far, wxo_near),
        query_nope,
        q_oth,
        qr_rows,
    )
    keys = ((2, KEYS, WIDE), BF)
    own_keys, own_stats = call(
        own_stats_kernel,
        [keys, ((2, 4, ROWS), F32)],
        5,
        smem=1,
        mega=8,
    )(info, early_far, early_near, late_far, late_near, qf)
    x_early_far, x_late_far, own_stats = fence(x_early_far, x_late_far, own_stats)
    across_keys, stats = call(
        all_stats_kernel,
        [keys, ((2, 8, ROWS), F32)],
        7,
        flops=3_000_000_000,
        smem=1,
        mega=8,
    )(info, x_early_far, x_early_near, x_late_far, x_late_near, qf, own_stats, delta)
    their_stats = swap(stats, "core")
    scratch = [pltpu.VMEM((2, WIDE, KEYS), BF), pltpu.VMEM((2, KEYS, WIDE), F32)]
    far, near, last, dq = call(
        across_kernel,
        [
            ((3, PACK, 128), BF),
            ((3, PACK, 128), BF),
            ((2, PACK, 128), BF),
            ((2, 2, WIDE, ROWS), BF),
        ],
        5,
        scratch,
        flops=10_000_000_000,
        smem=1,
        mega=12,
    )(info, across_keys, qf, g_rows, stats, their_stats)
    far, near, last = fence(far, near, last)
    far, near, last = shift_x(far, 1), shift_x(near, -1), shift_x(last, -1)
    own, dq_own, dq_send = call(
        own_kernel,
        [((8, PACK, 128), BF), ((2, ROWS, WIDE), BF), ((2, ROWS, WIDE), BF)],
        6,
        scratch,
        flops=20_000_000_000,
        smem=1,
        mega=16,
    )(info, own_keys, qf, g_rows, stats, their_stats, dq)
    far, near, own, dq_send = fence(far, near, own, dq_send)
    cross = dict(zip(OFFSETS, (*far, *near)))
    own = dict(zip(OFFSETS, own))
    mid = PACK // 2
    both = summed(own[4], cross[4]).astype(BF)
    up, down = shift(both[:mid], "z", 1), shift(both[mid:], "z", -1)
    dq_recv = swap(dq_send, "core")
    nope_grad, rope_grad, dw_own, dw_oth = call(
        query_kernel,
        [
            ((128, HEADS * NOPE), BF),
            ((128, HEADS * ROPE), BF),
            ((2, 8, 32, LAT), BF),
            ((2, 8, 32, LAT), BF),
        ],
        4,
        [pltpu.VMEM((HEADS * NOPE, LAT), BF)],
        smem=1,
    )(info, dq_own, dq_recv, w_full, query_nope)
    up, down, dw_oth = fence(up, down, dw_oth)
    fill = jnp.zeros((mid, 128), BF)
    up = shift(summed(own[3], cross[3], jnp.concatenate([up, fill])).astype(BF), "z", 1)
    down = shift(summed(own[5], cross[5], jnp.concatenate([fill, down])).astype(BF), "z", -1)
    dw_sum = summed(dw_own, swap(dw_oth, "core"))
    dw_mine, dw_recv = dw_sum[0], swap(dw_sum[1].astype(BF), "xl")
    up, down, dw_recv = fence(up, down, dw_recv)
    dw = summed(dw_mine, dw_recv)
    dw = {r: lax.dynamic_index_in_dim(dw, (z + r) & 7, 0, False) for r in range(8)}
    up = shift(joined(summed(own[2], cross[2], up), dw[4][:16]), "z", 1)
    down = shift(joined(summed(own[6], cross[6], down), dw[4][16:]), "z", -1)
    up, down, last = fence(up, down, last)
    cross.update(zip(OFFSETS[6:], last))
    dw_up = summed(dw[3], jnp.concatenate([up[PACK:].reshape(16, LAT), jnp.zeros((16, LAT), BF)]))
    dw_down = summed(dw[5], jnp.concatenate([jnp.zeros((16, LAT), BF), down[PACK:].reshape(16, LAT)]))
    up = shift(joined(summed(own[1], cross[1], up[:PACK]), dw_up), "z", 1)
    down = shift(joined(summed(own[7], cross[7], down[:PACK]), dw_down), "z", -1)
    up, down = fence(up, down)
    total = summed(own[0], cross[0], up[:PACK], down[:PACK])
    part = total.astype(BF)
    sides = [shift(part, "y", k) for k in (1, 2, 3)]
    dw_up = shift(summed(dw[2], up[PACK:].reshape(32, LAT)).astype(BF), "z", 1)
    dw_down = shift(summed(dw[6], down[PACK:].reshape(32, LAT)).astype(BF), "z", -1)
    *sides, dw_up, dw_down = fence(*sides, dw_up, dw_down)
    total = summed(total, *sides)
    other = swap(total.astype(BF), "xh")
    dw_up = shift(summed(dw[1], dw_up).astype(BF), "z", 1)
    dw_down = shift(summed(dw[7], dw_down).astype(BF), "z", -1)
    total = summed(total, other)
    dw_total = summed(dw[0], dw_up, dw_down)
    lat_grad = jnp.concatenate([total[128 * j : 128 * j + 128] for j in range(4)], axis=1)
    return lat_grad, total[512:576].T, nope_grad, rope_grad, dw_total


def solution(mesh):
    fine = Mesh(mesh.devices.reshape(2, 4, 2, 8, 2), ("xh", "y", "xl", "z", "core"))
    dp, ctx = ("xh", "y"), ("xl", "z", "core")
    return jax.shard_map(
        on_device,
        mesh=fine,
        in_specs=(
            P(ctx, dp),
            P(ctx, dp),
            P(ctx, None),
            P(ctx, None),
            P(ctx, dp),
            P(ctx, dp),
            P(dp + ctx, None),
        ),
        out_specs=(P(ctx, None), P(ctx, None), P(ctx, dp), P(ctx, dp), P(dp + ctx, None)),
        check_vma=False,
    )
```

```python
import math

import jax
import jax.numpy as jnp
from jax import lax
from jax.experimental import pallas as pl
from jax.experimental.pallas import tpu as pltpu
from jax.sharding import Mesh
from jax.sharding import PartitionSpec as P

NOPE = 128
ROPE = 64
LAT = 512
HEADS = 8
HALF = 64
ROWS = HEADS * HALF
WIDE = 640
PACK = 576
SCALE = 1.0 / math.sqrt(NOPE + ROPE)
LOG2E = math.log2(math.e)
LOW = -1e30
BF = jnp.bfloat16
F32 = jnp.float32
FAR, NEAR = (4, 3, 5), (2, 6, 1, 7, 0)
OFFSETS = FAR + NEAR
KEYS = len(OFFSETS) * HALF
MEGA = 1024 * 1024


def dot(a, b):
    return lax.dot_general(a, b, (((1,), (0,)), ((), ())), preferred_element_type=F32)


def dot_nt(a, b):
    return lax.dot_general(a, b, (((1,), (1,)), ((), ())), preferred_element_type=F32)


def call(kernel, outs, count, scratch=(), flops=0, smem=0, mega=6, space=pltpu.VMEM):
    vm = pl.BlockSpec(memory_space=pltpu.VMEM)
    sm = pl.BlockSpec(memory_space=pltpu.SMEM)
    return pl.pallas_call(
        kernel,
        out_shape=[jax.ShapeDtypeStruct(s, d) for s, d in outs],
        in_specs=[sm] * smem + [pl.BlockSpec(memory_space=space)] * count,
        out_specs=[vm] * len(outs),
        scratch_shapes=list(scratch),
        compiler_params=pltpu.CompilerParams(vmem_limit_bytes=mega * MEGA),
        cost_estimate=pl.CostEstimate(flops=flops, bytes_accessed=1_000, transcendentals=0),
    )


def pack_kernel(lat, rope, w, out, sems):
    copies = [pltpu.make_async_copy(rope, out.at[512:576], sems.at[8])]
    for j in range(4):
        part, rows = pl.ds(128 * j, 128), pl.ds(PACK + 32 * j, 32)
        copies.append(pltpu.make_async_copy(lat.at[:, part], out.at[part], sems.at[j]))
        copies.append(pltpu.make_async_copy(w.at[:, part], out.at[rows], sems.at[4 + j]))
    for copy in copies:
        copy.start()
    for copy in copies:
        copy.wait()


def unpack_kernel(*refs):
    packs, (early, late, w) = refs[:-3], refs[-3:]
    for b, pack in enumerate(packs):
        rows = pl.ds(b * HALF, HALF)
        for j in range(4):
            cols = pl.ds(128 * j, 128)
            early[rows, cols] = pack[pl.ds(128 * j, HALF), :]
            late[rows, cols] = pack[pl.ds(128 * j + HALF, HALF), :]
            w[b, :, cols] = pack[pl.ds(PACK + 32 * j, 32), :]
        ropes = jnp.concatenate(
            [pack[512:576, :].T, jnp.zeros((2 * HALF, 128 - ROPE), BF)], axis=1
        )
        early[rows, 512:640] = ropes[:HALF]
        late[rows, 512:640] = ropes[HALF:]


def prep_kernel(g, o, qr_own, qr_oth, qr_out, delta):
    zero = jnp.zeros((HALF, 128 - ROPE), BF)
    for part in range(2):
        rows = pl.ds(part * HALF, HALF)
        for p, qr in enumerate((qr_own, qr_oth)):
            for k in range(HEADS // 2):
                pair = qr[rows, pl.ds(128 * k, 128)]
                for i, ropes in enumerate((pair[:, :ROPE], pair[:, ROPE:])):
                    qr_out[part, p, pl.ds((2 * k + i) * HALF, HALF), :] = jnp.concatenate(
                        [ropes, zero], axis=1
                    )
        for k in range(HEADS // 2):
            halves = []
            for h in (2 * k, 2 * k + 1):
                cols = pl.ds(h * LAT, LAT)
                prod = g[rows, cols].astype(F32) * o[rows, cols].astype(F32)
                halves.append(
                    prod[:, 0:128] + prod[:, 128:256] + prod[:, 256:384] + prod[:, 384:512]
                )
            both = jnp.concatenate(halves, axis=0).T
            delta[pl.ds(part, 1), pl.ds(128 * k, 128)] = jnp.sum(both, axis=0, keepdims=True)


def put_rows(g_own, g_oth, rows):
    for p, g in enumerate((g_own, g_oth)):
        for part in range(2):
            for h in range(HEADS):
                rows[part, p, pl.ds(h * HALF, HALF), :] = g[
                    pl.ds(part * HALF, HALF), pl.ds(h * LAT, LAT)
                ]


def positions_of(info, p):
    core, z, xl = info[0], info[1], info[2]
    owner = 2 * (xl * 8 + z) + jnp.where(p == 0, core, 1 - core)
    early, late = [], []
    for r in OFFSETS:
        e = 2 * (xl * 8 + ((z + r) & 7)) + core
        early.append(e * HALF)
        late.append((63 - e) * HALF)
    return owner * HALF, (63 - owner) * HALF, early, late


def mask_of(first_row, key_rows):
    key = lax.broadcasted_iota(jnp.int32, (HALF, ROWS), 0)
    tok = lax.broadcasted_iota(jnp.int32, (HALF, ROWS), 1) & (HALF - 1)
    diff = key - tok
    return jnp.concatenate([diff <= first_row - k for k in key_rows], axis=0)


def stats_of(s):
    top = jnp.max(s, axis=0, keepdims=True)
    return top, jnp.sum(jnp.exp2(s - top), axis=0, keepdims=True)


def merge(a, b):
    top = jnp.maximum(a[0], b[0])
    return top, a[1] * jnp.exp2(a[0] - top) + b[1] * jnp.exp2(b[0] - top)


def latent_kernel(info, *refs):
    pieces, (q_own, q_oth, qr, w_full, qf) = refs[:8], refs[8:]
    core, z, xl = info[0], info[1], info[2]
    for i, (far, near) in enumerate(zip(pieces[0::2], pieces[1::2])):
        parity = core if i < 2 else 1 - core
        column = xl if i % 2 == 0 else 1 - xl
        for b, r in enumerate(OFFSETS):
            chip = column * 8 + ((z + r) & 7)
            at = pl.multiple_of((2 * chip + parity) * 32, 32)
            w_full[pl.ds(at, 32), :] = far[b] if b < len(FAR) else near[b - len(FAR)]
    for p, q in enumerate((q_own, q_oth)):
        for h in range(HEADS):
            lat = dot(q[:, pl.ds(h * NOPE, NOPE)], w_full[pl.ds(h * NOPE, NOPE), :]).astype(BF)
            qf[0, p, pl.ds(h * HALF, HALF), 0:512] = lat[:HALF]
            qf[1, p, pl.ds(h * HALF, HALF), 0:512] = lat[HALF:]
        for part in range(2):
            qf[part, p, :, 512:640] = qr[part, p]


def join_keys(parts, keys):
    count = len(FAR) * HALF
    for half in range(2):
        keys[half, 0:count, :] = parts[2 * half][...]
        keys[half, count:KEYS, :] = parts[2 * half + 1][...]


def own_stats_kernel(info, *refs):
    parts, (qf, keys, stats, s_early, s_late) = refs[:4], refs[4:]
    join_keys(parts, keys)
    factor = SCALE * LOG2E
    for p in range(2):
        first_early, first_late, early, late = positions_of(info, p)
        s = jnp.where(mask_of(first_early, early), dot_nt(keys[0], qf[0, p]) * factor, LOW)
        s_early[p] = s
        early_stats = stats_of(s)
        s = jnp.where(mask_of(first_late, late), dot_nt(keys[1], qf[1, p]) * factor, LOW)
        s_late[p, KEYS:, :] = s
        late_stats = stats_of(s)
        s = dot_nt(keys[0], qf[1, p]) * factor
        s_late[p, :KEYS, :] = s
        late_stats = merge(late_stats, stats_of(s))
        stats[p] = jnp.concatenate([*early_stats, *late_stats], axis=0)


def all_stats_kernel(info, *refs):
    parts, (qf, own, delta, keys, stats, s_late, s_cross) = refs[:4], refs[4:]
    join_keys(parts, keys)
    sel = 1 - info[2]
    factor = SCALE * LOG2E
    for p in range(2):
        s = dot_nt(keys[sel], qf[sel, p]) * factor
        s_cross[p] = s
        cross = stats_of(s)
        s = dot_nt(keys[0], qf[1, p]) * factor
        s_late[p] = s
        late = merge((own[p, 2:3], own[p, 3:4]), stats_of(s))
        early = (own[p, 0:1], own[p, 1:2])
        more_late, more_early = merge(late, cross), merge(early, cross)
        late = [jnp.where(sel == 1, a, b) for a, b in zip(more_late, late)]
        early = [jnp.where(sel == 0, a, b) for a, b in zip(more_early, early)]
        zero = jnp.zeros((2, ROWS), F32)
        stats[p] = jnp.concatenate([*early, *late, delta[...], zero], axis=0)


def row_terms(mine, theirs, p):
    a, b = mine[p], theirs[1 - p]
    lses, deltas = [], []
    for part in range(2):
        top, total = merge(
            (a[2 * part : 2 * part + 1], a[2 * part + 1 : 2 * part + 2]),
            (b[2 * part : 2 * part + 1], b[2 * part + 1 : 2 * part + 2]),
        )
        lses.append(top + jnp.log2(total))
        deltas.append((a if p == 0 else b)[4 + part : 5 + part])
    return lses, deltas


def block_grads(keys, s, queries, grads, lse, delta):
    prob = jnp.exp2(s - lse)
    dprob = dot_nt(keys[:, :LAT], grads)
    ds = ((prob * SCALE) * (dprob - delta)).astype(BF)
    return ds, dot(ds, queries), dot(prob.astype(BF), grads)


def add_grads(dk, at, full, lat):
    dk[at, :, 0:LAT] += full[:, :LAT] + lat
    dk[at, :, LAT:] += full[:, LAT:]


def put_grads(dk, b, out):
    rows = pl.ds(b * HALF, HALF)
    for j in range(4):
        cols = pl.ds(128 * j, 128)
        out[pl.ds(128 * j, HALF), :] = dk[0, rows, cols].astype(BF)
        out[pl.ds(128 * j + HALF, HALF), :] = dk[1, rows, cols].astype(BF)
    ropes = jnp.concatenate([dk[0, rows, 512:640], dk[1, rows, 512:640]], axis=0)
    out[512:576, :] = ropes.T[:ROPE].astype(BF)


def across_kernel(
    info, keys, s_late, s_cross, qf, g_own, g_oth, mine, theirs, far, near, last, dq, kt, dk, g
):
    put_rows(g_own, g_oth, g)
    sel = 1 - info[2]
    for i in range(2):
        kt[i] = keys[i].T
    dk[...] = jnp.zeros_like(dk)
    for p in range(2):
        lses, deltas = row_terms(mine, theirs, p)
        ds, full, lat = block_grads(keys[0], s_late[p], qf[1, p], g[1, p], lses[1], deltas[1])
        add_grads(dk, 0, full, lat)
        late = dot(kt[0], ds)
        lse = jnp.where(sel == 1, lses[1], lses[0])
        delta = jnp.where(sel == 1, deltas[1], deltas[0])
        ds, full, lat = block_grads(keys[sel], s_cross[p], qf[sel, p], g[sel, p], lse, delta)
        add_grads(dk, sel, full, lat)
        more = dot(kt[sel], ds)
        dq[1, p] = jnp.where(sel == 1, late + more, late).astype(BF)
        dq[0, p] = jnp.where(sel == 0, more, 0.0).astype(BF)
    for b in range(8):
        put_grads(dk, b, (far, near, last)[b // 3].at[b % 3])


def own_kernel(
    info, keys, s_early, s_late, qf, g_own, g_oth, mine, theirs, dq, *refs
):
    out, dq_own, dq_send, kt, dk, g = refs
    put_rows(g_own, g_oth, g)
    for i in range(2):
        kt[i] = keys[i].T
    dk[...] = jnp.zeros_like(dk)
    for p in range(2):
        lses, deltas = row_terms(mine, theirs, p)
        ds, full, lat = block_grads(
            keys[...].reshape(2 * KEYS, WIDE), s_late[p], qf[1, p], g[1, p], lses[1], deltas[1]
        )
        add_grads(dk, 0, full[:KEYS], lat[:KEYS])
        add_grads(dk, 1, full[KEYS:], lat[KEYS:])
        late = dq[1, p] + dot(kt[0], ds[:KEYS]) + dot(kt[1], ds[KEYS:])
        ds, full, lat = block_grads(
            keys[0], s_early[p], qf[0, p], g[0, p], lses[0], deltas[0]
        )
        add_grads(dk, 0, full, lat)
        early = dq[0, p] + dot(kt[0], ds)
        for part, value in enumerate((early, late)):
            if p == 0:
                dq_own[part] = value.T.astype(BF)
            else:
                dq_send[part] = value.T.astype(BF)
    for b in range(8):
        put_grads(dk, b, out.at[b])


def query_kernel(info, own, recv, w, q, nope, rope, dw_own, dw_oth, dw):
    def total(part, rows, cols):
        return (own[part, rows, cols].astype(F32) + recv[part, rows, cols].astype(F32)).astype(BF)

    pairs = []
    for h in range(HEADS):
        rows = pl.ds(h * HALF, HALF)
        lat = jnp.concatenate([total(part, rows, slice(0, LAT)) for part in range(2)], axis=0)
        weights = w[pl.ds(h * NOPE, NOPE), :]
        nope[:, pl.ds(h * NOPE, NOPE)] = dot_nt(lat, weights).astype(BF)
        dw[pl.ds(h * NOPE, NOPE), :] = dot(q[:, pl.ds(h * NOPE, NOPE)].T, lat).astype(BF)
        pairs.append(
            jnp.concatenate([total(part, rows, slice(512, 640)) for part in range(2)], axis=0)
        )
    for k in range(HEADS // 2):
        rope[:, pl.ds(128 * k, 128)] = jnp.concatenate(
            [pairs[2 * k][:, :ROPE], pairs[2 * k + 1][:, :ROPE]], axis=1
        )
    core, xl = info[0], info[2]
    for side in range(2):
        for z in range(8):
            chip = (xl if side == 0 else 1 - xl) * 8 + z
            for out, parity in ((dw_own, core), (dw_oth, 1 - core)):
                out[side, z] = dw[pl.ds(pl.multiple_of((2 * chip + parity) * 32, 32), 32), :]


def shift(x, axis, steps):
    n = lax.axis_size(axis)
    return lax.ppermute(x, axis, [(i, (i + steps) % n) for i in range(n)])


def swap(x, axis):
    return shift(x, axis, 1)


def summed(*xs):
    total = xs[0].astype(F32)
    for x in xs[1:]:
        total = total + x.astype(F32)
    return total


def fence(*xs):
    return lax.optimization_barrier(xs)


def joined(grads, dw):
    return jnp.concatenate([grads, dw.reshape(-1, 128)], axis=0).astype(BF)


def shift_x(x, steps):
    return lax.ppermute(x, ("xh", "xl"), [(i, (i + steps) % 4) for i in range(4)])


def on_device(query_nope, query_rope, latent, rope_key, grad_out, saved_out, up_key):
    core, z, xl = lax.axis_index("core"), lax.axis_index("z"), lax.axis_index("xl")
    info = jnp.stack([core, z, xl]).astype(jnp.int32)
    (packed,) = call(
        pack_kernel,
        [((PACK + 128, 128), BF)],
        3,
        [pltpu.SemaphoreType.DMA((9,))],
        mega=2,
        space=pl.ANY,
    )(latent, rope_key.T, up_key)

    def unpack(*packs):
        n = len(packs)
        rows = ((n * HALF, WIDE), BF)
        return call(unpack_kernel, [rows, rows, ((n, 32, LAT), BF)], n)(*packs)

    packed, grad_out, query_rope, query_nope = fence(packed, grad_out, query_rope, query_nope)
    u1, d1 = shift(packed, "z", 1), shift(packed, "z", -1)
    qr_oth, q_oth, g_oth = (swap(x, "core") for x in (query_rope, query_nope, grad_out))
    u1, d1, qr_oth, q_oth, g_oth = fence(u1, d1, qr_oth, q_oth, g_oth)
    u2, d2 = shift(u1, "z", 1), shift(d1, "z", -1)
    qr_rows, delta = call(
        prep_kernel, [((2, 2, ROWS, 128), BF), ((2, ROWS), F32)], 4
    )(grad_out, saved_out, query_rope, qr_oth)
    u2, d2, qr_rows, delta = fence(u2, d2, qr_rows, delta)
    u3, d3 = shift(u2, "z", 1), shift(d2, "z", -1)
    early_near, late_near, w_near = unpack(d2, u2, d1, u1, packed)
    wx_near, wo_near = swap(w_near, "xl"), swap(w_near, "core")
    x_early_near, x_late_near = shift_x(early_near, 1), shift_x(late_near, -1)
    u3, d3 = fence(u3, d3)
    u4 = shift(u3, "z", 1)
    u4, x_early_near, x_late_near = fence(u4, x_early_near, x_late_near)
    early_far, late_far, w_far = unpack(u4, d3, u3)
    wxo_near = swap(wx_near, "core")
    wx_far, wo_far = swap(w_far, "xl"), swap(w_far, "core")
    wxo_far = lax.ppermute(w_far, ("xl", "core"), [(i, 3 - i) for i in range(4)])
    x_early_far, x_late_far = shift_x(early_far, 1), shift_x(late_far, -1)
    w_full, qf = call(
        latent_kernel,
        [((HEADS * NOPE, LAT), BF), ((2, 2, ROWS, WIDE), BF)],
        11,
        smem=1,
    )(
        info,
        *(w_far, w_near, wx_far, wx_near, wo_far, wo_near, wxo_far, wxo_near),
        query_nope,
        q_oth,
        qr_rows,
    )
    keys = ((2, KEYS, WIDE), BF)
    own_keys, own_stats, *own_scores = call(
        own_stats_kernel,
        [keys, ((2, 4, ROWS), F32), ((2, KEYS, ROWS), F32), ((2, 2 * KEYS, ROWS), F32)],
        5,
        smem=1,
        mega=16,
    )(info, early_far, early_near, late_far, late_near, qf)
    x_early_far, x_late_far, own_stats = fence(x_early_far, x_late_far, own_stats)
    across_keys, stats, *across_scores = call(
        all_stats_kernel,
        [keys, ((2, 8, ROWS), F32), ((2, KEYS, ROWS), F32), ((2, KEYS, ROWS), F32)],
        7,
        flops=3_000_000_000,
        smem=1,
        mega=16,
    )(info, x_early_far, x_early_near, x_late_far, x_late_near, qf, own_stats, delta)
    their_stats = swap(stats, "core")
    scratch = [
        pltpu.VMEM((2, WIDE, KEYS), BF),
        pltpu.VMEM((2, KEYS, WIDE), F32),
        pltpu.VMEM((2, 2, ROWS, LAT), BF),
    ]
    far, near, last, dq = call(
        across_kernel,
        [
            ((3, PACK, 128), BF),
            ((3, PACK, 128), BF),
            ((2, PACK, 128), BF),
            ((2, 2, WIDE, ROWS), BF),
        ],
        8,
        scratch,
        flops=10_000_000_000,
        smem=1,
        mega=16,
    )(info, across_keys, *across_scores, qf, grad_out, g_oth, stats, their_stats)
    far, near, last = fence(far, near, last)
    far, near, last = shift_x(far, 1), shift_x(near, -1), shift_x(last, -1)
    own, dq_own, dq_send = call(
        own_kernel,
        [((8, PACK, 128), BF), ((2, ROWS, WIDE), BF), ((2, ROWS, WIDE), BF)],
        9,
        scratch,
        flops=20_000_000_000,
        smem=1,
        mega=20,
    )(info, own_keys, *own_scores, qf, grad_out, g_oth, stats, their_stats, dq)
    far, near, own, dq_send = fence(far, near, own, dq_send)
    cross = dict(zip(OFFSETS, (*far, *near)))
    own = dict(zip(OFFSETS, own))
    mid = PACK // 2
    both = summed(own[4], cross[4]).astype(BF)
    up, down = shift(both[:mid], "z", 1), shift(both[mid:], "z", -1)
    dq_recv = swap(dq_send, "core")
    nope_grad, rope_grad, dw_own, dw_oth = call(
        query_kernel,
        [
            ((128, HEADS * NOPE), BF),
            ((128, HEADS * ROPE), BF),
            ((2, 8, 32, LAT), BF),
            ((2, 8, 32, LAT), BF),
        ],
        4,
        [pltpu.VMEM((HEADS * NOPE, LAT), BF)],
        smem=1,
    )(info, dq_own, dq_recv, w_full, query_nope)
    up, down, dw_oth = fence(up, down, dw_oth)
    fill = jnp.zeros((mid, 128), BF)
    up = shift(summed(own[3], cross[3], jnp.concatenate([up, fill])).astype(BF), "z", 1)
    down = shift(summed(own[5], cross[5], jnp.concatenate([fill, down])).astype(BF), "z", -1)
    dw_sum = summed(dw_own, swap(dw_oth, "core"))
    dw_mine, dw_recv = dw_sum[0], swap(dw_sum[1].astype(BF), "xl")
    up, down, dw_recv = fence(up, down, dw_recv)
    dw = summed(dw_mine, dw_recv)
    dw = {r: lax.dynamic_index_in_dim(dw, (z + r) & 7, 0, False) for r in range(8)}
    up = shift(joined(summed(own[2], cross[2], up), dw[4][:16]), "z", 1)
    down = shift(joined(summed(own[6], cross[6], down), dw[4][16:]), "z", -1)
    up, down, last = fence(up, down, last)
    cross.update(zip(OFFSETS[6:], last))
    dw_up = summed(dw[3], jnp.concatenate([up[PACK:].reshape(16, LAT), jnp.zeros((16, LAT), BF)]))
    dw_down = summed(dw[5], jnp.concatenate([jnp.zeros((16, LAT), BF), down[PACK:].reshape(16, LAT)]))
    up = shift(joined(summed(own[1], cross[1], up[:PACK]), dw_up), "z", 1)
    down = shift(joined(summed(own[7], cross[7], down[:PACK]), dw_down), "z", -1)
    up, down = fence(up, down)
    total = summed(own[0], cross[0], up[:PACK], down[:PACK])
    part = total.astype(BF)
    sides = [shift(part, "y", k) for k in (1, 2, 3)]
    dw_up = shift(summed(dw[2], up[PACK:].reshape(32, LAT)).astype(BF), "z", 1)
    dw_down = shift(summed(dw[6], down[PACK:].reshape(32, LAT)).astype(BF), "z", -1)
    *sides, dw_up, dw_down = fence(*sides, dw_up, dw_down)
    total = summed(total, *sides)
    other = swap(total.astype(BF), "xh")
    dw_up = shift(summed(dw[1], dw_up).astype(BF), "z", 1)
    dw_down = shift(summed(dw[7], dw_down).astype(BF), "z", -1)
    total = summed(total, other)
    dw_total = summed(dw[0], dw_up, dw_down)
    lat_grad = jnp.concatenate([total[128 * j : 128 * j + 128] for j in range(4)], axis=1)
    return lat_grad, total[512:576].T, nope_grad, rope_grad, dw_total


def solution(mesh):
    fine = Mesh(mesh.devices.reshape(2, 4, 2, 8, 2), ("xh", "y", "xl", "z", "core"))
    dp, ctx = ("xh", "y"), ("xl", "z", "core")
    return jax.shard_map(
        on_device,
        mesh=fine,
        in_specs=(
            P(ctx, dp),
            P(ctx, dp),
            P(ctx, None),
            P(ctx, None),
            P(ctx, dp),
            P(ctx, dp),
            P(dp + ctx, None),
        ),
        out_specs=(P(ctx, None), P(ctx, None), P(ctx, dp), P(ctx, dp), P(dp + ctx, None)),
        check_vma=False,
    )
```

```python
import math

import jax
import jax.numpy as jnp
from jax import lax
from jax.experimental import pallas as pl
from jax.experimental.pallas import tpu as pltpu
from jax.sharding import Mesh
from jax.sharding import PartitionSpec as P

NOPE = 128
ROPE = 64
LAT = 512
HEADS = 8
HALF = 64
ROWS = HEADS * HALF
WIDE = 640
PACK = 576
SCALE = 1.0 / math.sqrt(NOPE + ROPE)
LOG2E = math.log2(math.e)
LOW = -1e30
BF = jnp.bfloat16
F32 = jnp.float32
BATCHES = ((4,), (3, 5), (2, 6), (1, 7, 0))
FAR, NEAR = BATCHES[0] + BATCHES[1], BATCHES[2] + BATCHES[3]
OFFSETS = FAR + NEAR
KEYS = len(OFFSETS) * HALF
MEGA = 1024 * 1024


def dot(a, b):
    return lax.dot_general(a, b, (((1,), (0,)), ((), ())), preferred_element_type=F32)


def dot_nt(a, b):
    return lax.dot_general(a, b, (((1,), (1,)), ((), ())), preferred_element_type=F32)


def call(kernel, outs, count, scratch=(), flops=0, smem=0, mega=6, space=pltpu.VMEM):
    vm = pl.BlockSpec(memory_space=pltpu.VMEM)
    sm = pl.BlockSpec(memory_space=pltpu.SMEM)
    return pl.pallas_call(
        kernel,
        out_shape=[jax.ShapeDtypeStruct(s, d) for s, d in outs],
        in_specs=[sm] * smem + [pl.BlockSpec(memory_space=space)] * count,
        out_specs=[vm] * len(outs),
        scratch_shapes=list(scratch),
        compiler_params=pltpu.CompilerParams(vmem_limit_bytes=mega * MEGA),
        cost_estimate=pl.CostEstimate(flops=flops, bytes_accessed=1_000, transcendentals=0),
    )


def pack_kernel(lat, rope, w, out, sems):
    copies = [pltpu.make_async_copy(rope, out.at[512:576], sems.at[8])]
    for j in range(4):
        part, rows = pl.ds(128 * j, 128), pl.ds(PACK + 32 * j, 32)
        copies.append(pltpu.make_async_copy(lat.at[:, part], out.at[part], sems.at[j]))
        copies.append(pltpu.make_async_copy(w.at[:, part], out.at[rows], sems.at[4 + j]))
    for copy in copies:
        copy.start()
    for copy in copies:
        copy.wait()


def unpack_kernel(first, *refs):
    packs, (here, there, w) = refs[:-3], refs[-3:]
    for b, pack in enumerate(packs):
        keys = here if b < first else there
        rows = pl.ds((b if b < first else b - first) * HALF, HALF)
        for j in range(4):
            cols = pl.ds(128 * j, 128)
            keys[0, rows, cols] = pack[pl.ds(128 * j, HALF), :]
            keys[1, rows, cols] = pack[pl.ds(128 * j + HALF, HALF), :]
            w[b, :, cols] = pack[pl.ds(PACK + 32 * j, 32), :]
        ropes = jnp.concatenate(
            [pack[512:576, :].T, jnp.zeros((2 * HALF, 128 - ROPE), BF)], axis=1
        )
        keys[0, rows, 512:640] = ropes[:HALF]
        keys[1, rows, 512:640] = ropes[HALF:]


def prep_kernel(g, o, qr_own, qr_oth, qr_out, delta):
    zero = jnp.zeros((HALF, 128 - ROPE), BF)
    for part in range(2):
        rows = pl.ds(part * HALF, HALF)
        for p, qr in enumerate((qr_own, qr_oth)):
            for k in range(HEADS // 2):
                pair = qr[rows, pl.ds(128 * k, 128)]
                for i, ropes in enumerate((pair[:, :ROPE], pair[:, ROPE:])):
                    qr_out[part, p, pl.ds((2 * k + i) * HALF, HALF), :] = jnp.concatenate(
                        [ropes, zero], axis=1
                    )
        for k in range(HEADS // 2):
            halves = []
            for h in (2 * k, 2 * k + 1):
                cols = pl.ds(h * LAT, LAT)
                prod = g[rows, cols].astype(F32) * o[rows, cols].astype(F32)
                halves.append(
                    prod[:, 0:128] + prod[:, 128:256] + prod[:, 256:384] + prod[:, 384:512]
                )
            both = jnp.concatenate(halves, axis=0).T
            delta[pl.ds(part, 1), pl.ds(128 * k, 128)] = jnp.sum(both, axis=0, keepdims=True)


def put_rows(g_own, g_oth, rows):
    for p, g in enumerate((g_own, g_oth)):
        for part in range(2):
            for h in range(HEADS):
                rows[part, p, pl.ds(h * HALF, HALF), :] = g[
                    pl.ds(part * HALF, HALF), pl.ds(h * LAT, LAT)
                ]


def positions_of(info, p):
    core, z, xl = info[0], info[1], info[2]
    owner = 2 * (xl * 8 + z) + jnp.where(p == 0, core, 1 - core)
    early, late = [], []
    for r in OFFSETS:
        e = 2 * (xl * 8 + ((z + r) & 7)) + core
        early.append(e * HALF)
        late.append((63 - e) * HALF)
    return owner * HALF, (63 - owner) * HALF, early, late


def mask_of(first_row, key_rows):
    key = lax.broadcasted_iota(jnp.int32, (HALF, ROWS), 0)
    tok = lax.broadcasted_iota(jnp.int32, (HALF, ROWS), 1) & (HALF - 1)
    diff = key - tok
    return jnp.concatenate([diff <= first_row - k for k in key_rows], axis=0)


def stats_of(s):
    top = jnp.max(s, axis=0, keepdims=True)
    return top, jnp.sum(jnp.exp2(s - top), axis=0, keepdims=True)


def merge(a, b):
    top = jnp.maximum(a[0], b[0])
    return top, a[1] * jnp.exp2(a[0] - top) + b[1] * jnp.exp2(b[0] - top)


def latent_kernel(info, *refs):
    pieces, (q_own, q_oth, qr, w_full, qf) = refs[:8], refs[8:]
    core, z, xl = info[0], info[1], info[2]
    for i, (far, near) in enumerate(zip(pieces[0::2], pieces[1::2])):
        parity = core if i < 2 else 1 - core
        column = xl if i % 2 == 0 else 1 - xl
        for b, r in enumerate(OFFSETS):
            chip = column * 8 + ((z + r) & 7)
            at = pl.multiple_of((2 * chip + parity) * 32, 32)
            w_full[pl.ds(at, 32), :] = far[b] if b < len(FAR) else near[b - len(FAR)]
    for p, q in enumerate((q_own, q_oth)):
        for h in range(HEADS):
            lat = dot(q[:, pl.ds(h * NOPE, NOPE)], w_full[pl.ds(h * NOPE, NOPE), :]).astype(BF)
            qf[0, p, pl.ds(h * HALF, HALF), 0:512] = lat[:HALF]
            qf[1, p, pl.ds(h * HALF, HALF), 0:512] = lat[HALF:]
        for part in range(2):
            qf[part, p, :, 512:640] = qr[part, p]


def join_keys(parts, keys):
    at = 0
    for part, offsets in zip(parts, BATCHES):
        count = len(offsets) * HALF
        for half in range(2):
            keys[half, at : at + count, :] = part[half]
        at += count


def own_stats_kernel(info, *refs):
    parts, (qf, keys, stats, s_early, s_late) = refs[:4], refs[4:]
    join_keys(parts, keys)
    factor = SCALE * LOG2E
    for p in range(2):
        first_early, first_late, early, late = positions_of(info, p)
        s = jnp.where(mask_of(first_early, early), dot_nt(keys[0], qf[0, p]) * factor, LOW)
        s_early[p] = s
        early_stats = stats_of(s)
        s = jnp.where(mask_of(first_late, late), dot_nt(keys[1], qf[1, p]) * factor, LOW)
        s_late[p, KEYS:, :] = s
        late_stats = stats_of(s)
        s = dot_nt(keys[0], qf[1, p]) * factor
        s_late[p, :KEYS, :] = s
        late_stats = merge(late_stats, stats_of(s))
        stats[p] = jnp.concatenate([*early_stats, *late_stats], axis=0)


def all_stats_kernel(info, *refs):
    parts, (qf, own, delta, keys, stats, s_late, s_cross) = refs[:4], refs[4:]
    join_keys(parts, keys)
    sel = 1 - info[2]
    factor = SCALE * LOG2E
    for p in range(2):
        s = dot_nt(keys[sel], qf[sel, p]) * factor
        s_cross[p] = s
        cross = stats_of(s)
        s = dot_nt(keys[0], qf[1, p]) * factor
        s_late[p] = s
        late = merge((own[p, 2:3], own[p, 3:4]), stats_of(s))
        early = (own[p, 0:1], own[p, 1:2])
        more_late, more_early = merge(late, cross), merge(early, cross)
        late = [jnp.where(sel == 1, a, b) for a, b in zip(more_late, late)]
        early = [jnp.where(sel == 0, a, b) for a, b in zip(more_early, early)]
        zero = jnp.zeros((2, ROWS), F32)
        stats[p] = jnp.concatenate([*early, *late, delta[...], zero], axis=0)


def row_terms(mine, theirs, p):
    a, b = mine[p], theirs[1 - p]
    lses, deltas = [], []
    for part in range(2):
        top, total = merge(
            (a[2 * part : 2 * part + 1], a[2 * part + 1 : 2 * part + 2]),
            (b[2 * part : 2 * part + 1], b[2 * part + 1 : 2 * part + 2]),
        )
        lses.append(top + jnp.log2(total))
        deltas.append((a if p == 0 else b)[4 + part : 5 + part])
    return lses, deltas


def block_grads(keys, s, queries, grads, lse, delta):
    prob = jnp.exp2(s - lse)
    dprob = dot_nt(keys[:, :LAT], grads)
    ds = ((prob * SCALE) * (dprob - delta)).astype(BF)
    return ds, dot(ds, queries), dot(prob.astype(BF), grads)


def add_grads(dk, at, full, lat):
    dk[at, :, 0:LAT] += full[:, :LAT] + lat
    dk[at, :, LAT:] += full[:, LAT:]


def put_grads(dk, b, out):
    rows = pl.ds(b * HALF, HALF)
    for j in range(4):
        cols = pl.ds(128 * j, 128)
        out[pl.ds(128 * j, HALF), :] = dk[0, rows, cols].astype(BF)
        out[pl.ds(128 * j + HALF, HALF), :] = dk[1, rows, cols].astype(BF)
    ropes = jnp.concatenate([dk[0, rows, 512:640], dk[1, rows, 512:640]], axis=0)
    out[512:576, :] = ropes.T[:ROPE].astype(BF)


def across_kernel(
    info, keys, s_late, s_cross, qf, g_own, g_oth, mine, theirs, far, near, last, dq, kt, dk, g
):
    put_rows(g_own, g_oth, g)
    sel = 1 - info[2]
    for i in range(2):
        kt[i] = keys[i].T
    dk[...] = jnp.zeros_like(dk)
    for p in range(2):
        lses, deltas = row_terms(mine, theirs, p)
        ds, full, lat = block_grads(keys[0], s_late[p], qf[1, p], g[1, p], lses[1], deltas[1])
        add_grads(dk, 0, full, lat)
        late = dot(kt[0], ds)
        lse = jnp.where(sel == 1, lses[1], lses[0])
        delta = jnp.where(sel == 1, deltas[1], deltas[0])
        ds, full, lat = block_grads(keys[sel], s_cross[p], qf[sel, p], g[sel, p], lse, delta)
        add_grads(dk, sel, full, lat)
        more = dot(kt[sel], ds)
        dq[1, p] = jnp.where(sel == 1, late + more, late).astype(BF)
        dq[0, p] = jnp.where(sel == 0, more, 0.0).astype(BF)
    for b in range(8):
        put_grads(dk, b, (far, near, last)[b // 3].at[b % 3])


def own_kernel(
    info, keys, s_early, s_late, qf, g_own, g_oth, mine, theirs, dq, *refs
):
    out, dq_own, dq_send, kt, dk, g = refs
    put_rows(g_own, g_oth, g)
    for i in range(2):
        kt[i] = keys[i].T
    dk[...] = jnp.zeros_like(dk)
    for p in range(2):
        lses, deltas = row_terms(mine, theirs, p)
        ds, full, lat = block_grads(
            keys[...].reshape(2 * KEYS, WIDE), s_late[p], qf[1, p], g[1, p], lses[1], deltas[1]
        )
        add_grads(dk, 0, full[:KEYS], lat[:KEYS])
        add_grads(dk, 1, full[KEYS:], lat[KEYS:])
        late = dq[1, p] + dot(kt[0], ds[:KEYS]) + dot(kt[1], ds[KEYS:])
        ds, full, lat = block_grads(
            keys[0], s_early[p], qf[0, p], g[0, p], lses[0], deltas[0]
        )
        add_grads(dk, 0, full, lat)
        early = dq[0, p] + dot(kt[0], ds)
        for part, value in enumerate((early, late)):
            if p == 0:
                dq_own[part] = value.T.astype(BF)
            else:
                dq_send[part] = value.T.astype(BF)
    for b in range(8):
        put_grads(dk, b, out.at[b])


def query_kernel(info, own, recv, w, q, nope, rope, dw_own, dw_oth, dw):
    def total(part, rows, cols):
        return (own[part, rows, cols].astype(F32) + recv[part, rows, cols].astype(F32)).astype(BF)

    pairs = []
    for h in range(HEADS):
        rows = pl.ds(h * HALF, HALF)
        lat = jnp.concatenate([total(part, rows, slice(0, LAT)) for part in range(2)], axis=0)
        weights = w[pl.ds(h * NOPE, NOPE), :]
        nope[:, pl.ds(h * NOPE, NOPE)] = dot_nt(lat, weights).astype(BF)
        dw[pl.ds(h * NOPE, NOPE), :] = dot(q[:, pl.ds(h * NOPE, NOPE)].T, lat).astype(BF)
        pairs.append(
            jnp.concatenate([total(part, rows, slice(512, 640)) for part in range(2)], axis=0)
        )
    for k in range(HEADS // 2):
        rope[:, pl.ds(128 * k, 128)] = jnp.concatenate(
            [pairs[2 * k][:, :ROPE], pairs[2 * k + 1][:, :ROPE]], axis=1
        )
    core, xl = info[0], info[2]
    for side in range(2):
        for z in range(8):
            chip = (xl if side == 0 else 1 - xl) * 8 + z
            for out, parity in ((dw_own, core), (dw_oth, 1 - core)):
                out[side, z] = dw[pl.ds(pl.multiple_of((2 * chip + parity) * 32, 32), 32), :]


def final_kernel(total, other, lat, rope):
    for j in range(4):
        rows = pl.ds(128 * j, 128)
        lat[:, rows] = total[rows, :] + other[rows, :].astype(F32)
    rope[...] = total[512:576, :] + other[512:576, :].astype(F32)


def shift(x, axis, steps):
    n = lax.axis_size(axis)
    return lax.ppermute(x, axis, [(i, (i + steps) % n) for i in range(n)])


def swap(x, axis):
    return shift(x, axis, 1)


def summed(*xs):
    total = xs[0].astype(F32)
    for x in xs[1:]:
        total = total + x.astype(F32)
    return total


def fence(*xs):
    return lax.optimization_barrier(xs)


def joined(grads, dw):
    return jnp.concatenate([grads, dw.reshape(-1, 128)], axis=0).astype(BF)


def shift_x(x, steps):
    return lax.ppermute(x, ("xh", "xl"), [(i, (i + steps) % 4) for i in range(4)])


def on_device(query_nope, query_rope, latent, rope_key, grad_out, saved_out, up_key):
    core, z, xl = lax.axis_index("core"), lax.axis_index("z"), lax.axis_index("xl")
    info = jnp.stack([core, z, xl]).astype(jnp.int32)
    (packed,) = call(
        pack_kernel,
        [((PACK + 128, 128), BF)],
        3,
        [pltpu.SemaphoreType.DMA((9,))],
        mega=2,
        space=pl.ANY,
    )(latent, rope_key.T, up_key)

    def unpack(first, *packs):
        n = len(packs)
        outs = [((2, k * HALF, WIDE), BF) for k in (first, n - first)] + [((n, 32, LAT), BF)]

        def kernel(*refs):
            unpack_kernel(first, *refs)

        return call(kernel, outs, n)(*packs)

    def across(here, there):
        return swap(here, "xl"), lax.ppermute(there, ("xh", "xl"), [(i, 3 - i) for i in range(4)])

    packed, grad_out, query_rope, query_nope = fence(packed, grad_out, query_rope, query_nope)
    u1, d1 = shift(packed, "z", 1), shift(packed, "z", -1)
    qr_oth, q_oth, g_oth = (swap(x, "core") for x in (query_rope, query_nope, grad_out))
    u1, d1, qr_oth, q_oth, g_oth = fence(u1, d1, qr_oth, q_oth, g_oth)
    u2, d2 = shift(u1, "z", 1), shift(d1, "z", -1)
    qr_rows, delta = call(
        prep_kernel, [((2, 2, ROWS, 128), BF), ((2, ROWS), F32)], 4
    )(grad_out, saved_out, query_rope, qr_oth)
    u2, d2, qr_rows, delta = fence(u2, d2, qr_rows, delta)
    u3, d3 = shift(u2, "z", 1), shift(d2, "z", -1)
    *near, w_near = unpack(2, d2, u2, d1, u1, packed)
    x_near = across(*near)
    wx_near, wo_near = swap(w_near, "xl"), swap(w_near, "core")
    u3, d3 = fence(u3, d3)
    u4 = shift(u3, "z", 1)
    u4, wx_near, *x_near = fence(u4, wx_near, *x_near)
    *far, w_far = unpack(1, u4, d3, u3)
    wxo_near = swap(wx_near, "core")
    wx_far, wo_far = swap(w_far, "xl"), swap(w_far, "core")
    x_far = across(*far)
    wxo_far = swap(wx_far, "core")
    w_full, qf = call(
        latent_kernel,
        [((HEADS * NOPE, LAT), BF), ((2, 2, ROWS, WIDE), BF)],
        11,
        smem=1,
    )(
        info,
        *(w_far, w_near, wx_far, wx_near, wo_far, wo_near, wxo_far, wxo_near),
        query_nope,
        q_oth,
        qr_rows,
    )
    keys = ((2, KEYS, WIDE), BF)
    own_keys, own_stats, *own_scores = call(
        own_stats_kernel,
        [keys, ((2, 4, ROWS), F32), ((2, KEYS, ROWS), F32), ((2, 2 * KEYS, ROWS), F32)],
        5,
        smem=1,
        mega=16,
    )(info, *far, *near, qf)
    *x_far, own_stats = fence(*x_far, own_stats)
    across_keys, stats, *across_scores = call(
        all_stats_kernel,
        [keys, ((2, 8, ROWS), F32), ((2, KEYS, ROWS), F32), ((2, KEYS, ROWS), F32)],
        7,
        flops=3_000_000_000,
        smem=1,
        mega=16,
    )(info, *x_far, *x_near, qf, own_stats, delta)
    their_stats = swap(stats, "core")
    scratch = [
        pltpu.VMEM((2, WIDE, KEYS), BF),
        pltpu.VMEM((2, KEYS, WIDE), F32),
        pltpu.VMEM((2, 2, ROWS, LAT), BF),
    ]
    far, near, last, dq = call(
        across_kernel,
        [
            ((3, PACK, 128), BF),
            ((3, PACK, 128), BF),
            ((2, PACK, 128), BF),
            ((2, 2, WIDE, ROWS), BF),
        ],
        8,
        scratch,
        flops=10_000_000_000,
        smem=1,
        mega=16,
    )(info, across_keys, *across_scores, qf, grad_out, g_oth, stats, their_stats)
    far, near, last = fence(far, near, last)
    far, near, last = shift_x(far, 1), shift_x(near, -1), shift_x(last, -1)
    own, dq_own, dq_send = call(
        own_kernel,
        [((8, PACK, 128), BF), ((2, ROWS, WIDE), BF), ((2, ROWS, WIDE), BF)],
        9,
        scratch,
        flops=20_000_000_000,
        smem=1,
        mega=20,
    )(info, own_keys, *own_scores, qf, grad_out, g_oth, stats, their_stats, dq)
    far, near, own, dq_send = fence(far, near, own, dq_send)
    cross = dict(zip(OFFSETS, (*far, *near)))
    own = dict(zip(OFFSETS, own))
    mid = PACK // 2
    both = summed(own[4], cross[4]).astype(BF)
    up, down = shift(both[:mid], "z", 1), shift(both[mid:], "z", -1)
    dq_recv = swap(dq_send, "core")
    nope_grad, rope_grad, dw_own, dw_oth = call(
        query_kernel,
        [
            ((128, HEADS * NOPE), BF),
            ((128, HEADS * ROPE), BF),
            ((2, 8, 32, LAT), BF),
            ((2, 8, 32, LAT), BF),
        ],
        4,
        [pltpu.VMEM((HEADS * NOPE, LAT), BF)],
        smem=1,
    )(info, dq_own, dq_recv, w_full, query_nope)
    up, down, dw_oth = fence(up, down, dw_oth)
    fill = jnp.zeros((mid, 128), BF)
    up = shift(summed(own[3], cross[3], jnp.concatenate([up, fill])).astype(BF), "z", 1)
    down = shift(summed(own[5], cross[5], jnp.concatenate([fill, down])).astype(BF), "z", -1)
    dw_sum = summed(dw_own, swap(dw_oth, "core"))
    dw_mine, dw_recv = dw_sum[0], swap(dw_sum[1].astype(BF), "xl")
    up, down, dw_recv = fence(up, down, dw_recv)
    dw = summed(dw_mine, dw_recv)
    dw = {r: lax.dynamic_index_in_dim(dw, (z + r) & 7, 0, False) for r in range(8)}
    up = shift(joined(summed(own[2], cross[2], up), dw[4][:16]), "z", 1)
    down = shift(joined(summed(own[6], cross[6], down), dw[4][16:]), "z", -1)
    up, down, last = fence(up, down, last)
    cross.update(zip(OFFSETS[6:], last))
    dw_up = summed(dw[3], jnp.concatenate([up[PACK:].reshape(16, LAT), jnp.zeros((16, LAT), BF)]))
    dw_down = summed(dw[5], jnp.concatenate([jnp.zeros((16, LAT), BF), down[PACK:].reshape(16, LAT)]))
    up = shift(joined(summed(own[1], cross[1], up[:PACK]), dw_up), "z", 1)
    down = shift(joined(summed(own[7], cross[7], down[:PACK]), dw_down), "z", -1)
    up, down = fence(up, down)
    total = summed(own[0], cross[0], up[:PACK], down[:PACK])
    part = total.astype(BF)
    sides = [shift(part, "y", k) for k in (1, 2, 3)]
    dw_up = shift(summed(dw[2], up[PACK:].reshape(32, LAT)).astype(BF), "z", 1)
    dw_down = shift(summed(dw[6], down[PACK:].reshape(32, LAT)).astype(BF), "z", -1)
    *sides, dw_up, dw_down = fence(*sides, dw_up, dw_down)
    total = summed(total, *sides)
    other = swap(total.astype(BF), "xh")
    dw_up = shift(summed(dw[1], dw_up).astype(BF), "z", 1)
    dw_down = shift(summed(dw[7], dw_down).astype(BF), "z", -1)
    lat_grad, rope_grad_t = call(final_kernel, [((128, LAT), F32), ((ROPE, 128), F32)], 2)(
        total, other
    )
    dw_total = summed(dw[0], dw_up, dw_down)
    return lat_grad, rope_grad_t.T, nope_grad, rope_grad, dw_total


def solution(mesh):
    fine = Mesh(mesh.devices.reshape(2, 4, 2, 8, 2), ("xh", "y", "xl", "z", "core"))
    dp, ctx = ("xh", "y"), ("xl", "z", "core")
    return jax.shard_map(
        on_device,
        mesh=fine,
        in_specs=(
            P(ctx, dp),
            P(ctx, dp),
            P(ctx, None),
            P(ctx, None),
            P(ctx, dp),
            P(ctx, dp),
            P(dp + ctx, None),
        ),
        out_specs=(P(ctx, None), P(ctx, None), P(ctx, dp), P(ctx, dp), P(dp + ctx, None)),
        check_vma=False,
    )
```

```python
import math

import jax
import jax.numpy as jnp
from jax import lax
from jax.experimental import pallas as pl
from jax.experimental.pallas import tpu as pltpu
from jax.sharding import Mesh
from jax.sharding import PartitionSpec as P

NOPE = 128
ROPE = 64
LAT = 512
HEADS = 8
HALF = 64
ROWS = HEADS * HALF
WIDE = 640
PACK = 576
SCALE = 1.0 / math.sqrt(NOPE + ROPE)
LOG2E = math.log2(math.e)
LOW = -1e30
BF = jnp.bfloat16
F32 = jnp.float32
BATCHES = ((4,), (3, 5), (2, 6), (1, 7, 0))
FAR, NEAR = BATCHES[0] + BATCHES[1], BATCHES[2] + BATCHES[3]
OFFSETS = FAR + NEAR
KEYS = len(OFFSETS) * HALF
MEGA = 1024 * 1024


def dot(a, b):
    return lax.dot_general(a, b, (((1,), (0,)), ((), ())), preferred_element_type=F32)


def dot_nt(a, b):
    return lax.dot_general(a, b, (((1,), (1,)), ((), ())), preferred_element_type=F32)


def call(kernel, outs, count, scratch=(), flops=0, smem=0, mega=6, space=pltpu.VMEM):
    vm = pl.BlockSpec(memory_space=pltpu.VMEM)
    sm = pl.BlockSpec(memory_space=pltpu.SMEM)
    return pl.pallas_call(
        kernel,
        out_shape=[jax.ShapeDtypeStruct(s, d) for s, d in outs],
        in_specs=[sm] * smem + [pl.BlockSpec(memory_space=space)] * count,
        out_specs=[vm] * len(outs),
        scratch_shapes=list(scratch),
        compiler_params=pltpu.CompilerParams(vmem_limit_bytes=mega * MEGA),
        cost_estimate=pl.CostEstimate(flops=flops, bytes_accessed=1_000, transcendentals=0),
    )


def pack_kernel(lat, rope, w, out, sems):
    copies = [pltpu.make_async_copy(rope, out.at[512:576], sems.at[8])]
    for j in range(4):
        part, rows = pl.ds(128 * j, 128), pl.ds(PACK + 32 * j, 32)
        copies.append(pltpu.make_async_copy(lat.at[:, part], out.at[part], sems.at[j]))
        copies.append(pltpu.make_async_copy(w.at[:, part], out.at[rows], sems.at[4 + j]))
    for copy in copies:
        copy.start()
    for copy in copies:
        copy.wait()


def unpack_kernel(first, *refs):
    packs, (here, there, w) = refs[:-3], refs[-3:]
    for b, pack in enumerate(packs):
        keys = here if b < first else there
        rows = pl.ds((b if b < first else b - first) * HALF, HALF)
        for j in range(4):
            cols = pl.ds(128 * j, 128)
            keys[rows, cols] = pack[pl.ds(128 * j, HALF), :]
            keys[rows, pl.ds(LAT + 128 * j, 128)] = pack[pl.ds(128 * j + HALF, HALF), :]
            w[b, :, cols] = pack[pl.ds(PACK + 32 * j, 32), :]
        ropes = pack[512:576, :].T
        keys[rows, 1024:1152] = jnp.concatenate([ropes[:HALF], ropes[HALF:]], axis=1)


def prep_kernel(g, o, qr_own, qr_oth, qr_out, delta):
    zero = jnp.zeros((HALF, 128 - ROPE), BF)
    for part in range(2):
        rows = pl.ds(part * HALF, HALF)
        for p, qr in enumerate((qr_own, qr_oth)):
            for k in range(HEADS // 2):
                pair = qr[rows, pl.ds(128 * k, 128)]
                for i, ropes in enumerate((pair[:, :ROPE], pair[:, ROPE:])):
                    qr_out[part, p, pl.ds((2 * k + i) * HALF, HALF), :] = jnp.concatenate(
                        [ropes, zero], axis=1
                    )
        for k in range(HEADS // 2):
            halves = []
            for h in (2 * k, 2 * k + 1):
                cols = pl.ds(h * LAT, LAT)
                prod = g[rows, cols].astype(F32) * o[rows, cols].astype(F32)
                halves.append(
                    prod[:, 0:128] + prod[:, 128:256] + prod[:, 256:384] + prod[:, 384:512]
                )
            both = jnp.concatenate(halves, axis=0).T
            delta[pl.ds(part, 1), pl.ds(128 * k, 128)] = jnp.sum(both, axis=0, keepdims=True)


def put_rows(g_own, g_oth, rows):
    for p, g in enumerate((g_own, g_oth)):
        for part in range(2):
            for h in range(HEADS):
                rows[part, p, pl.ds(h * HALF, HALF), :] = g[
                    pl.ds(part * HALF, HALF), pl.ds(h * LAT, LAT)
                ]


def positions_of(info, p):
    core, z, xl = info[0], info[1], info[2]
    owner = 2 * (xl * 8 + z) + jnp.where(p == 0, core, 1 - core)
    early, late = [], []
    for r in OFFSETS:
        e = 2 * (xl * 8 + ((z + r) & 7)) + core
        early.append(e * HALF)
        late.append((63 - e) * HALF)
    return owner * HALF, (63 - owner) * HALF, early, late


def mask_of(first_row, key_rows):
    key = lax.broadcasted_iota(jnp.int32, (HALF, ROWS), 0)
    tok = lax.broadcasted_iota(jnp.int32, (HALF, ROWS), 1) & (HALF - 1)
    diff = key - tok
    return jnp.concatenate([diff <= first_row - k for k in key_rows], axis=0)


def stats_of(s):
    top = jnp.max(s, axis=0, keepdims=True)
    return top, jnp.sum(jnp.exp2(s - top), axis=0, keepdims=True)


def merge(a, b):
    top = jnp.maximum(a[0], b[0])
    return top, a[1] * jnp.exp2(a[0] - top) + b[1] * jnp.exp2(b[0] - top)


def latent_kernel(info, *refs):
    pieces, (q_own, q_oth, qr, w_full, qf) = refs[:8], refs[8:]
    core, z, xl = info[0], info[1], info[2]
    for i, (far, near) in enumerate(zip(pieces[0::2], pieces[1::2])):
        parity = core if i < 2 else 1 - core
        column = xl if i % 2 == 0 else 1 - xl
        for b, r in enumerate(OFFSETS):
            chip = column * 8 + ((z + r) & 7)
            at = pl.multiple_of((2 * chip + parity) * 32, 32)
            w_full[pl.ds(at, 32), :] = far[b] if b < len(FAR) else near[b - len(FAR)]
    for p, q in enumerate((q_own, q_oth)):
        for h in range(HEADS):
            lat = dot(q[:, pl.ds(h * NOPE, NOPE)], w_full[pl.ds(h * NOPE, NOPE), :]).astype(BF)
            qf[0, p, pl.ds(h * HALF, HALF), 0:512] = lat[:HALF]
            qf[1, p, pl.ds(h * HALF, HALF), 0:512] = lat[HALF:]
        for part in range(2):
            qf[part, p, :, 512:640] = qr[part, p]


def join_keys(parts, keys):
    at = 0
    for part, offsets in zip(parts, BATCHES):
        count = len(offsets) * HALF
        rows = pl.ds(at, count)
        keys[0, rows, 0:LAT] = part[:, 0:LAT]
        keys[1, rows, 0:LAT] = part[:, LAT : 2 * LAT]
        ropes = part[:, 1024:1152]
        keys[0, rows, LAT:WIDE] = ropes
        keys[1, rows, LAT:WIDE] = jnp.concatenate([ropes[:, ROPE:], ropes[:, :ROPE]], axis=1)
        at += count


def own_stats_kernel(info, *refs):
    parts, (qf, keys, stats, s_early, s_late) = refs[:4], refs[4:]
    join_keys(parts, keys)
    factor = SCALE * LOG2E
    for p in range(2):
        first_early, first_late, early, late = positions_of(info, p)
        s = jnp.where(mask_of(first_early, early), dot_nt(keys[0], qf[0, p]) * factor, LOW)
        s_early[p] = s
        early_stats = stats_of(s)
        s = jnp.where(mask_of(first_late, late), dot_nt(keys[1], qf[1, p]) * factor, LOW)
        s_late[p, KEYS:, :] = s
        late_stats = stats_of(s)
        s = dot_nt(keys[0], qf[1, p]) * factor
        s_late[p, :KEYS, :] = s
        late_stats = merge(late_stats, stats_of(s))
        stats[p] = jnp.concatenate([*early_stats, *late_stats], axis=0)


def all_stats_kernel(info, *refs):
    parts, (qf, own, delta, keys, stats, s_late, s_cross) = refs[:4], refs[4:]
    join_keys(parts, keys)
    sel = 1 - info[2]
    factor = SCALE * LOG2E
    for p in range(2):
        s = dot_nt(keys[sel], qf[sel, p]) * factor
        s_cross[p] = s
        cross = stats_of(s)
        s = dot_nt(keys[0], qf[1, p]) * factor
        s_late[p] = s
        late = merge((own[p, 2:3], own[p, 3:4]), stats_of(s))
        early = (own[p, 0:1], own[p, 1:2])
        more_late, more_early = merge(late, cross), merge(early, cross)
        late = [jnp.where(sel == 1, a, b) for a, b in zip(more_late, late)]
        early = [jnp.where(sel == 0, a, b) for a, b in zip(more_early, early)]
        zero = jnp.zeros((2, ROWS), F32)
        stats[p] = jnp.concatenate([*early, *late, delta[...], zero], axis=0)


def row_terms(mine, theirs, p):
    a, b = mine[p], theirs[1 - p]
    lses, deltas = [], []
    for part in range(2):
        top, total = merge(
            (a[2 * part : 2 * part + 1], a[2 * part + 1 : 2 * part + 2]),
            (b[2 * part : 2 * part + 1], b[2 * part + 1 : 2 * part + 2]),
        )
        lses.append(top + jnp.log2(total))
        deltas.append((a if p == 0 else b)[4 + part : 5 + part])
    return lses, deltas


def block_grads(keys, s, queries, grads, lse, delta):
    prob = jnp.exp2(s - lse)
    dprob = dot_nt(keys[:, :LAT], grads)
    ds = ((prob * SCALE) * (dprob - delta)).astype(BF)
    return ds, dot(ds, queries), dot(prob.astype(BF), grads)


def add_grads(dk, at, full, lat):
    dk[at, :, 0:LAT] += full[:, :LAT] + lat
    dk[at, :, LAT:] += full[:, LAT:]


def put_grads(dk, b, out):
    rows = pl.ds(b * HALF, HALF)
    for j in range(4):
        cols = pl.ds(128 * j, 128)
        out[pl.ds(128 * j, HALF), :] = dk[0, rows, cols].astype(BF)
        out[pl.ds(128 * j + HALF, HALF), :] = dk[1, rows, cols].astype(BF)
    ropes = jnp.concatenate([dk[0, rows, 512:640], dk[1, rows, 512:640]], axis=0)
    out[512:576, :] = ropes.T[:ROPE].astype(BF)


def across_kernel(
    info, keys, s_late, s_cross, qf, g_own, g_oth, mine, theirs, far, near, last, dq, kt, dk, g
):
    put_rows(g_own, g_oth, g)
    sel = 1 - info[2]
    for i in range(2):
        kt[i] = keys[i].T
    dk[...] = jnp.zeros_like(dk)
    for p in range(2):
        lses, deltas = row_terms(mine, theirs, p)
        ds, full, lat = block_grads(keys[0], s_late[p], qf[1, p], g[1, p], lses[1], deltas[1])
        add_grads(dk, 0, full, lat)
        late = dot(kt[0], ds)
        lse = jnp.where(sel == 1, lses[1], lses[0])
        delta = jnp.where(sel == 1, deltas[1], deltas[0])
        ds, full, lat = block_grads(keys[sel], s_cross[p], qf[sel, p], g[sel, p], lse, delta)
        add_grads(dk, sel, full, lat)
        more = dot(kt[sel], ds)
        dq[1, p] = jnp.where(sel == 1, late + more, late).astype(BF)
        dq[0, p] = jnp.where(sel == 0, more, 0.0).astype(BF)
    for b in range(8):
        put_grads(dk, b, (far, near, last)[b // 3].at[b % 3])


def own_kernel(
    info, keys, s_early, s_late, qf, g_own, g_oth, mine, theirs, dq, *refs
):
    out, dq_own, dq_send, kt, dk, g = refs
    put_rows(g_own, g_oth, g)
    for i in range(2):
        kt[i] = keys[i].T
    dk[...] = jnp.zeros_like(dk)
    for p in range(2):
        lses, deltas = row_terms(mine, theirs, p)
        ds, full, lat = block_grads(
            keys[...].reshape(2 * KEYS, WIDE), s_late[p], qf[1, p], g[1, p], lses[1], deltas[1]
        )
        add_grads(dk, 0, full[:KEYS], lat[:KEYS])
        add_grads(dk, 1, full[KEYS:], lat[KEYS:])
        late = dq[1, p] + dot(kt[0], ds[:KEYS]) + dot(kt[1], ds[KEYS:])
        ds, full, lat = block_grads(
            keys[0], s_early[p], qf[0, p], g[0, p], lses[0], deltas[0]
        )
        add_grads(dk, 0, full, lat)
        early = dq[0, p] + dot(kt[0], ds)
        for part, value in enumerate((early, late)):
            if p == 0:
                dq_own[part] = value.T.astype(BF)
            else:
                dq_send[part] = value.T.astype(BF)
    for b in range(8):
        put_grads(dk, b, out.at[b])


def query_kernel(info, own, recv, w, q, nope, rope, dw_own, dw_oth, dw):
    def total(part, rows, cols):
        return (own[part, rows, cols].astype(F32) + recv[part, rows, cols].astype(F32)).astype(BF)

    pairs = []
    for h in range(HEADS):
        rows = pl.ds(h * HALF, HALF)
        lat = jnp.concatenate([total(part, rows, slice(0, LAT)) for part in range(2)], axis=0)
        weights = w[pl.ds(h * NOPE, NOPE), :]
        nope[:, pl.ds(h * NOPE, NOPE)] = dot_nt(lat, weights).astype(BF)
        dw[pl.ds(h * NOPE, NOPE), :] = dot(q[:, pl.ds(h * NOPE, NOPE)].T, lat).astype(BF)
        pairs.append(
            jnp.concatenate([total(part, rows, slice(512, 640)) for part in range(2)], axis=0)
        )
    for k in range(HEADS // 2):
        rope[:, pl.ds(128 * k, 128)] = jnp.concatenate(
            [pairs[2 * k][:, :ROPE], pairs[2 * k + 1][:, :ROPE]], axis=1
        )
    core, xl = info[0], info[2]
    for side in range(2):
        for z in range(8):
            chip = (xl if side == 0 else 1 - xl) * 8 + z
            for out, parity in ((dw_own, core), (dw_oth, 1 - core)):
                out[side, z] = dw[pl.ds(pl.multiple_of((2 * chip + parity) * 32, 32), 32), :]


def final_kernel(total, other, lat, rope):
    for j in range(4):
        rows = pl.ds(128 * j, 128)
        lat[:, rows] = total[rows, :] + other[rows, :].astype(F32)
    rope[...] = total[512:576, :] + other[512:576, :].astype(F32)


def shift(x, axis, steps):
    n = lax.axis_size(axis)
    return lax.ppermute(x, axis, [(i, (i + steps) % n) for i in range(n)])


def swap(x, axis):
    return shift(x, axis, 1)


def summed(*xs):
    total = xs[0].astype(F32)
    for x in xs[1:]:
        total = total + x.astype(F32)
    return total


def fence(*xs):
    return lax.optimization_barrier(xs)


def joined(grads, dw):
    return jnp.concatenate([grads, dw.reshape(-1, 128)], axis=0).astype(BF)


def shift_x(x, steps):
    return lax.ppermute(x, ("xh", "xl"), [(i, (i + steps) % 4) for i in range(4)])


def on_device(query_nope, query_rope, latent, rope_key, grad_out, saved_out, up_key):
    core, z, xl = lax.axis_index("core"), lax.axis_index("z"), lax.axis_index("xl")
    info = jnp.stack([core, z, xl]).astype(jnp.int32)
    (packed,) = call(
        pack_kernel,
        [((PACK + 128, 128), BF)],
        3,
        [pltpu.SemaphoreType.DMA((9,))],
        mega=2,
        space=pl.ANY,
    )(latent, rope_key.T, up_key)

    def unpack(first, *packs):
        n = len(packs)
        outs = [((k * HALF, 2 * LAT + 128), BF) for k in (first, n - first)] + [((n, 32, LAT), BF)]

        def kernel(*refs):
            unpack_kernel(first, *refs)

        return call(kernel, outs, n)(*packs)

    def across(here, there):
        return swap(here, "xl"), lax.ppermute(there, ("xh", "xl"), [(i, 3 - i) for i in range(4)])

    packed, grad_out, query_rope, query_nope = fence(packed, grad_out, query_rope, query_nope)
    u1, d1 = shift(packed, "z", 1), shift(packed, "z", -1)
    qr_oth, q_oth, g_oth = (swap(x, "core") for x in (query_rope, query_nope, grad_out))
    u1, d1, qr_oth, q_oth, g_oth = fence(u1, d1, qr_oth, q_oth, g_oth)
    u2, d2 = shift(u1, "z", 1), shift(d1, "z", -1)
    qr_rows, delta = call(
        prep_kernel, [((2, 2, ROWS, 128), BF), ((2, ROWS), F32)], 4
    )(grad_out, saved_out, query_rope, qr_oth)
    u2, d2, qr_rows, delta = fence(u2, d2, qr_rows, delta)
    u3, d3 = shift(u2, "z", 1), shift(d2, "z", -1)
    *near, w_near = unpack(2, d2, u2, d1, u1, packed)
    x_near = across(*near)
    wx_near, wo_near = swap(w_near, "xl"), swap(w_near, "core")
    u3, d3 = fence(u3, d3)
    u4 = shift(u3, "z", 1)
    u4, wx_near, *x_near = fence(u4, wx_near, *x_near)
    *far, w_far = unpack(1, u4, d3, u3)
    wxo_near = swap(wx_near, "core")
    wx_far, wo_far = swap(w_far, "xl"), swap(w_far, "core")
    x_far = across(*far)
    wxo_far = swap(wx_far, "core")
    w_full, qf = call(
        latent_kernel,
        [((HEADS * NOPE, LAT), BF), ((2, 2, ROWS, WIDE), BF)],
        11,
        smem=1,
    )(
        info,
        *(w_far, w_near, wx_far, wx_near, wo_far, wo_near, wxo_far, wxo_near),
        query_nope,
        q_oth,
        qr_rows,
    )
    keys = ((2, KEYS, WIDE), BF)
    own_keys, own_stats, *own_scores = call(
        own_stats_kernel,
        [keys, ((2, 4, ROWS), F32), ((2, KEYS, ROWS), F32), ((2, 2 * KEYS, ROWS), F32)],
        5,
        smem=1,
        mega=16,
    )(info, *far, *near, qf)
    *x_far, own_stats = fence(*x_far, own_stats)
    across_keys, stats, *across_scores = call(
        all_stats_kernel,
        [keys, ((2, 8, ROWS), F32), ((2, KEYS, ROWS), F32), ((2, KEYS, ROWS), F32)],
        7,
        flops=3_000_000_000,
        smem=1,
        mega=16,
    )(info, *x_far, *x_near, qf, own_stats, delta)
    their_stats = swap(stats, "core")
    scratch = [
        pltpu.VMEM((2, WIDE, KEYS), BF),
        pltpu.VMEM((2, KEYS, WIDE), F32),
        pltpu.VMEM((2, 2, ROWS, LAT), BF),
    ]
    far, near, last, dq = call(
        across_kernel,
        [
            ((3, PACK, 128), BF),
            ((3, PACK, 128), BF),
            ((2, PACK, 128), BF),
            ((2, 2, WIDE, ROWS), BF),
        ],
        8,
        scratch,
        flops=10_000_000_000,
        smem=1,
        mega=16,
    )(info, across_keys, *across_scores, qf, grad_out, g_oth, stats, their_stats)
    far, near, last = fence(far, near, last)
    far, near, last = shift_x(far, 1), shift_x(near, -1), shift_x(last, -1)
    own, dq_own, dq_send = call(
        own_kernel,
        [((8, PACK, 128), BF), ((2, ROWS, WIDE), BF), ((2, ROWS, WIDE), BF)],
        9,
        scratch,
        flops=20_000_000_000,
        smem=1,
        mega=20,
    )(info, own_keys, *own_scores, qf, grad_out, g_oth, stats, their_stats, dq)
    far, near, own, dq_send = fence(far, near, own, dq_send)
    cross = dict(zip(OFFSETS, (*far, *near)))
    own = dict(zip(OFFSETS, own))
    mid = PACK // 2
    both = summed(own[4], cross[4]).astype(BF)
    up, down = shift(both[:mid], "z", 1), shift(both[mid:], "z", -1)
    dq_recv = swap(dq_send, "core")
    nope_grad, rope_grad, dw_own, dw_oth = call(
        query_kernel,
        [
            ((128, HEADS * NOPE), BF),
            ((128, HEADS * ROPE), BF),
            ((2, 8, 32, LAT), BF),
            ((2, 8, 32, LAT), BF),
        ],
        4,
        [pltpu.VMEM((HEADS * NOPE, LAT), BF)],
        smem=1,
    )(info, dq_own, dq_recv, w_full, query_nope)
    up, down, dw_oth = fence(up, down, dw_oth)
    fill = jnp.zeros((mid, 128), BF)
    up = shift(summed(own[3], cross[3], jnp.concatenate([up, fill])).astype(BF), "z", 1)
    down = shift(summed(own[5], cross[5], jnp.concatenate([fill, down])).astype(BF), "z", -1)
    dw_sum = summed(dw_own, swap(dw_oth, "core"))
    dw_mine, dw_recv = dw_sum[0], swap(dw_sum[1].astype(BF), "xl")
    up, down, dw_recv = fence(up, down, dw_recv)
    dw = summed(dw_mine, dw_recv)
    dw = {r: lax.dynamic_index_in_dim(dw, (z + r) & 7, 0, False) for r in range(8)}
    up = shift(joined(summed(own[2], cross[2], up), dw[4][:16]), "z", 1)
    down = shift(joined(summed(own[6], cross[6], down), dw[4][16:]), "z", -1)
    up, down, last = fence(up, down, last)
    cross.update(zip(OFFSETS[6:], last))
    dw_up = summed(dw[3], jnp.concatenate([up[PACK:].reshape(16, LAT), jnp.zeros((16, LAT), BF)]))
    dw_down = summed(dw[5], jnp.concatenate([jnp.zeros((16, LAT), BF), down[PACK:].reshape(16, LAT)]))
    up = shift(joined(summed(own[1], cross[1], up[:PACK]), dw_up), "z", 1)
    down = shift(joined(summed(own[7], cross[7], down[:PACK]), dw_down), "z", -1)
    up, down = fence(up, down)
    total = summed(own[0], cross[0], up[:PACK], down[:PACK])
    part = total.astype(BF)
    sides = [shift(part, "y", k) for k in (1, 2, 3)]
    dw_up = shift(summed(dw[2], up[PACK:].reshape(32, LAT)).astype(BF), "z", 1)
    dw_down = shift(summed(dw[6], down[PACK:].reshape(32, LAT)).astype(BF), "z", -1)
    *sides, dw_up, dw_down = fence(*sides, dw_up, dw_down)
    total = summed(total, *sides)
    other = swap(total.astype(BF), "xh")
    dw_up = shift(summed(dw[1], dw_up).astype(BF), "z", 1)
    dw_down = shift(summed(dw[7], dw_down).astype(BF), "z", -1)
    lat_grad, rope_grad_t = call(final_kernel, [((128, LAT), F32), ((ROPE, 128), F32)], 2)(
        total, other
    )
    dw_total = summed(dw[0], dw_up, dw_down)
    return lat_grad, rope_grad_t.T, nope_grad, rope_grad, dw_total


def solution(mesh):
    fine = Mesh(mesh.devices.reshape(2, 4, 2, 8, 2), ("xh", "y", "xl", "z", "core"))
    dp, ctx = ("xh", "y"), ("xl", "z", "core")
    return jax.shard_map(
        on_device,
        mesh=fine,
        in_specs=(
            P(ctx, dp),
            P(ctx, dp),
            P(ctx, None),
            P(ctx, None),
            P(ctx, dp),
            P(ctx, dp),
            P(dp + ctx, None),
        ),
        out_specs=(P(ctx, None), P(ctx, None), P(ctx, dp), P(ctx, dp), P(dp + ctx, None)),
        check_vma=False,
    )
```
